512 devices in a mesh: group: 8 (over x, z_hi), rollout: 64 (over y, z_lo, core).
Axes of the slice: x: 4, y: 4, z: 16 (z_hi: 2, z_lo: 8; z = z_hi * 8 + z_lo), core: 2. Of those that a mesh axis runs over, the one named last changes fastest.
Arguments:
- queries: bfloat16 [65536, 2048], P(('group', 'rollout')), parts along dimension 0, may hold values from -120 to 120
- roll_kv: bfloat16 [2, 65536, 512], P(None, ('group', 'rollout')), parts along dimension 1, may hold values from -6 to 6
- prefix_kv: bfloat16 [4096, 2, 512], P(('group', 'rollout')), parts along dimension 0, may hold values from -6.2 to 6.2
- grad_seed: bfloat16 [65536, 2048], P(('group', 'rollout')), parts along dimension 0, may hold values from -6 to 6
- lengths: int32 [512], P(('group', 'rollout')), parts along dimension 0, may hold values from 1 to 128, 6144 in all
- rewards: int32 [512], P(('group', 'rollout')), parts along dimension 0, may hold values from 10 to 70
Outputs:
- grad_queries: bfloat16 [65536, 2048], P(('group', 'rollout')), parts along dimension 0
- grad_roll_kv: bfloat16 [2, 65536, 512], P(None, ('group', 'rollout')), parts along dimension 1
- grad_prefix_kv: bfloat16 [4096, 2, 512], P(('group', 'rollout')), parts along dimension 0
The draws below stay inside these ranges and needn't reach their ends.
There are 8 independent parts, one for each index of `group`. The reference program is written for one: setup_inputs(seed, part) draws one part's arguments, and reference() takes and returns one part's arrays. A program takes and returns all parts, laid end to end along the dimension named above; each array names one. Nothing has to cross between parts.
All inputs are finite; a program needn't handle non-finite values. No bound on the sum of `lengths` on one device may be relied on, other than what follows from the above.
Results may differ from the reference program's by a relative error of at most 0.0095.
Values may be sent and summed in bfloat16 or wider, within the bound.
A program may use at most 64 MiB of HBM per device.

```python
import math
import jax
import jax.numpy as jnp
import numpy as np
from jax import lax

HQ = 16
HK = 4
HD = 128
R_MAX = 128
PREFIX = 512
TOKS = 8192
N_ROLLOUT = 64


def base_keys(key):
    return jnp.clip(jax.random.normal(key, (PREFIX, HK * HD), jnp.float32), -6.0, 6.0)


def draw_prefix_kv(key, part):
    shared = base_keys(key)
    key = jax.random.fold_in(key, 5)
    values = jnp.clip(jax.random.normal(key, (PREFIX, HK * HD), jnp.float32), -6.0, 6.0)
    return jnp.stack([shared, values], axis=1).astype(jnp.bfloat16)


def draw_queries(key, part):
    key = jax.random.fold_in(key, 3)
    filled = jnp.clip(jax.random.normal(key, (TOKS, HQ * HD), jnp.float32) * 1.5, -9.0, 9.0)
    return filled.astype(jnp.bfloat16)


def draw_rewards(key, part):
    key = jax.random.fold_in(key, 7)
    rollout_total = TOKS // R_MAX
    row_index = jnp.arange(rollout_total)
    ramp = 10 + 40 * row_index // max(rollout_total - 1, 1)
    noise = jax.random.randint(key, (rollout_total,), 0, 21)
    noise = jnp.where(row_index == 0, 0, jnp.where(row_index == rollout_total - 1, 20, noise))
    return (ramp + noise).astype(jnp.int32)


def steps_of(own_key, extent, shards, smallest, high):
    def one(axis_at, parts):
        heights = jax.random.uniform(jax.random.fold_in(jax.random.fold_in(own_key, 6), axis_at), (parts,), jnp.float32, smallest / len(shards), high / len(shards))
        return jnp.repeat(jnp.exp(heights), extent[axis_at] // parts).reshape((-1,) + (1,) * (len(extent) - axis_at - 1))

    loudness = one(*shards[0])
    for cut in shards[1:]:
        loudness = loudness * one(*cut)
    return loudness


def split_up(count, total, limit, slope):
    weights = [(1 << 20) // math.isqrt(standing ** slope) + 1 for standing in range(2, count + 1)]
    spare, holding = total - limit - (count - 1), [1] * (count - 1)
    while spare > 0:
        movable = [i for i in range(count - 1) if holding[i] < limit]
        whole, budget = sum([weights[i] for i in movable]), spare
        for i in movable:
            more = min(limit - holding[i], max(1, budget * weights[i] // whole), spare)
            holding[i] = holding[i] + more
            spare = spare - more
    return np.array([limit] + holding)


def ragged(stream_key, amount, total, bound, lean):
    if amount == 2:
        one = jax.random.randint(stream_key, (), max(1, total - bound), min(bound, total - 1) + 1)
        return jnp.stack([one, total - one])
    tallies = jnp.asarray(split_up(amount, total, bound, lean), jnp.int32)
    couples = (amount - 1) // 2
    giver, taker = tallies[1:1 + 2 * couples:2], tallies[2:2 + 2 * couples:2]
    margin = jnp.minimum(giver - 1, bound - taker)
    shifted = jax.random.randint(jax.random.fold_in(stream_key, 1), (couples,), 0, 1 << 20) % (margin + 1)
    tallies = tallies.at[1:1 + 2 * couples:2].set(giver - shifted).at[2:2 + 2 * couples:2].set(taker + shifted)
    return tallies[jax.random.permutation(jax.random.fold_in(stream_key, 2), amount)]


def normal_values(rng, extent, scale, most, shards=(), held_as=jnp.bfloat16):
    array = jax.random.normal(rng, extent, jnp.float32) * scale
    if len(shards) > 0:
        array = steps_of(rng, extent, shards, -0.22, 0.18) * array
    return jnp.clip(array, min=-most, max=most).astype(held_as)


def setup_inputs(seed: int = 0, part: int = 0) -> dict:
    key_list = jax.random.split(jax.random.key(seed), 7)
    own_keys = jax.random.split(jax.random.fold_in(key_list[6], part), 7)
    queries = draw_queries(jax.random.fold_in(jax.random.fold_in(key_list[6], part), 71), part)
    roll_kv = normal_values(own_keys[1], (2, TOKS, HK * HD), 1.0, 6.0, ((1, 64),))
    prefix_kv = draw_prefix_kv(jax.random.fold_in(jax.random.fold_in(key_list[6], part), 71), part)
    grad_seed = normal_values(own_keys[3], (TOKS, HQ * HD), 1.0, 6.0, ((0, 64),))
    lengths = ragged(own_keys[4], N_ROLLOUT, TOKS * 3 // 4, R_MAX, 1).astype(jnp.int32)
    rewards = draw_rewards(jax.random.fold_in(jax.random.fold_in(key_list[6], part), 71), part)
    return dict(queries=queries, roll_kv=roll_kv, prefix_kv=prefix_kv, grad_seed=grad_seed, lengths=lengths, rewards=rewards)


def rollout_grads(query_rows, roll_pair, prefix_pair, seed_rows, length, weight):
    row_count = query_rows.shape[0]
    prefix_rows = prefix_pair.shape[0]
    group_size = HQ // HK
    score_scale = 1.0 / math.sqrt(HD)
    all_keys = jnp.concatenate([prefix_pair[:, 0], roll_pair[0]], axis=0).astype(jnp.float32).reshape(-1, HK, HD)
    all_values = jnp.concatenate([prefix_pair[:, 1], roll_pair[1]], axis=0).astype(jnp.float32).reshape(-1, HK, HD)
    query_f32 = query_rows.astype(jnp.float32).reshape(row_count, HK, group_size, HD)
    position = jnp.arange(row_count, dtype=jnp.int32)
    column = jnp.arange(prefix_rows + row_count, dtype=jnp.int32)
    allowed = (column[None, :] < prefix_rows) | (column[None, :] - prefix_rows <= position[:, None])
    live_row = position < length
    grad_out = jnp.where(live_row[:, None], weight * seed_rows.astype(jnp.float32), 0.0)
    grad_bf = lax.optimization_barrier(grad_out.astype(jnp.bfloat16)).astype(jnp.float32)
    grad_bf = grad_bf.reshape(row_count, HK, group_size, HD)
    scores = jnp.einsum('tkgd,nkd->kgtn', query_f32, all_keys) * score_scale
    scores = jnp.where(allowed, scores, -1e+30)
    row_max = lax.optimization_barrier(jnp.max(scores, axis=-1, keepdims=True))
    log_total = row_max + jnp.log(lax.optimization_barrier(jnp.sum(jnp.exp(scores - row_max), axis=-1, keepdims=True)))
    softmax = jnp.exp(scores - log_total)
    soft_bf = lax.optimization_barrier(softmax.astype(jnp.bfloat16)).astype(jnp.float32)
    attended = jnp.einsum('kgtn,nkd->kgtd', soft_bf, all_values)
    row_dot = jnp.einsum('tkgd,kgtd->kgt', grad_bf, attended)[..., None]
    grad_soft = jnp.einsum('tkgd,nkd->kgtn', grad_bf, all_values)
    grad_score = softmax * (grad_soft - row_dot)
    score_bf = lax.optimization_barrier(grad_score.astype(jnp.bfloat16)).astype(jnp.float32)
    grad_query = jnp.einsum('kgtn,nkd->tkgd', score_bf, all_keys) * score_scale
    grad_query = grad_query.reshape(row_count, HQ * HD).astype(jnp.bfloat16)
    grad_key = (jnp.einsum('kgtn,tkgd->nkd', score_bf, query_f32) * score_scale).reshape(-1, HK * HD)
    grad_value = jnp.einsum('kgtn,tkgd->nkd', soft_bf, grad_bf).reshape(-1, HK * HD)
    prefix_term = jnp.stack([grad_key[:prefix_rows], grad_value[:prefix_rows]], axis=1)
    own_grads = jnp.stack([grad_key[prefix_rows:], grad_value[prefix_rows:]], axis=0).astype(jnp.bfloat16)
    return (grad_query, own_grads, prefix_term)

def reference(queries, roll_kv, prefix_kv, grad_seed, lengths, rewards):
    reward_vals = rewards.astype(jnp.float32)
    reward_mean = jnp.sum(reward_vals) / N_ROLLOUT
    reward_var = jnp.sum(reward_vals * reward_vals) / N_ROLLOUT - reward_mean * reward_mean
    reward_std = jnp.sqrt(reward_var)
    token_total = jnp.sum(lengths.astype(jnp.float32))
    token_weight = (reward_vals - reward_mean) / (reward_std + 1.0) * (float(N_ROLLOUT * R_MAX) / token_total)
    query_split = queries.reshape(N_ROLLOUT, R_MAX, HQ * HD)
    seed_split = grad_seed.reshape(N_ROLLOUT, R_MAX, HQ * HD)
    pair_split = roll_kv.reshape(2, N_ROLLOUT, R_MAX, HK * HD).transpose(1, 0, 2, 3)

    def scan_step(summed, slices):
        query_rows, roll_pair, seed_rows, length, weight = slices
        grad_query, own_grads, prefix_term = rollout_grads(query_rows, roll_pair, prefix_kv, seed_rows, length, weight)
        return (summed + prefix_term, (grad_query, own_grads))
    start_sum = jnp.zeros((PREFIX, 2, HK * HD), jnp.float32)
    summed, (query_grads, pair_grads) = lax.scan(scan_step, start_sum, (query_split, pair_split, seed_split, lengths, token_weight))
    grad_queries = query_grads.reshape(TOKS, HQ * HD)
    grad_roll_kv = pair_grads.transpose(1, 0, 2, 3).reshape(2, TOKS, HK * HD)
    return (grad_queries, grad_roll_kv, summed.astype(jnp.bfloat16))
```

```python
import functools
import math

import jax
import jax.numpy as jnp
from jax import lax
from jax.experimental import pallas as pl
from jax.experimental.pallas import tpu as pltpu
from jax.sharding import PartitionSpec as P

HD = 128
GROUP = 4
NY = 4
NZ = 8
ROWS = 128
SCALE = 1.0 / math.sqrt(HD)
LOG2E = 1.4426950408889634
MESH = pl.DeviceIdType.MESH
F32 = jnp.float32
BF16 = jnp.bfloat16
NT = (((1,), (1,)), ((), ()))
TN = (((0,), (0,)), ((), ()))


def dot(a, b, dims=(((1,), (0,)), ((), ()))):
    return lax.dot_general(a, b, dims, preferred_element_type=F32)


def kernel(
    q_hbm, rkv_hbm, pkv_ref, do_hbm, len_ref, rew_ref,
    gq_hbm, grkv_hbm, gp_ref,
    kvblk, zrecv, kv_all, stat_own, statz, staty_own, staty,
    q_in, do_in, rkv_in, qcat, docat, p_sc, ds_sc,
    ysend, yrecv, yown, zsend, zback, gq_st, grkv_st,
    zs_sem, zr_sem, ss_sem, sr_sem, ys_sem, yr_sem, sys_sem, syr_sem,
    in_sem, xs_sem, xr_sem, rys_sem, ryr_sem, rzs_sem, rzr_sem, out_sem, os_sem, or_sem,
):
    group = lax.axis_index("group")
    index = lax.axis_index("rollout")
    y = index // (2 * NZ)
    z = (index // 2) % NZ
    core = index % 2
    other = 1 - core
    prefix = NY * NZ * 16

    def device(yy, zz, cc):
        return (group, (yy * NZ + zz) * 2 + cc)

    def remote(src, dst, ssem, rsem, where):
        return pltpu.make_async_remote_copy(
            src_ref=src, dst_ref=dst, send_sem=ssem, recv_sem=rsem,
            device_id=where, device_id_type=MESH,
        )

    column = [(d, e) for d in range(NZ) for e in range(2) if d or e]

    def peer(d, e):
        return device(y, z ^ d, core ^ e)

    barrier = pltpu.get_barrier_semaphore()
    for d, e in column:
        pl.semaphore_signal(barrier, inc=1, device_id=peer(d, e), device_id_type=MESH)
    for d in range(1, NY):
        pl.semaphore_signal(
            barrier, inc=1, device_id=device((y + d) % NY, z, core), device_id_type=MESH
        )

    my_q = pl.multiple_of(core * 1024, 1024)
    other_q = pl.multiple_of(other * 1024, 1024)
    my_kv = pl.multiple_of(core * 256, 256)
    other_kv = pl.multiple_of(other * 256, 256)
    loads = [
        pltpu.make_async_copy(q_hbm.at[:, pl.ds(my_q, 1024)], q_in.at[core], in_sem.at[0]),
        pltpu.make_async_copy(do_hbm.at[:, pl.ds(my_q, 1024)], do_in.at[core], in_sem.at[1]),
        pltpu.make_async_copy(rkv_hbm.at[:, :, pl.ds(my_kv, 256)], rkv_in.at[core], in_sem.at[2]),
    ]
    for load in loads:
        load.start()

    pair = pkv_ref[...].astype(F32)
    own_k = pair[:, 0, :]
    own_v = pair[:, 1, :]
    for cc in range(2):
        cols = slice(cc * 256, cc * 256 + 256)
        kvblk[cc] = jnp.concatenate([own_k[:, cols], own_v[:, cols]], axis=0).astype(BF16)
    zrecv[z * 2 + core] = kvblk[core]

    lane = lax.broadcasted_iota(jnp.int32, (1, 128), 1)
    reward = rew_ref[0].astype(F32)
    length = len_ref[0].astype(F32)
    stat = jnp.where(
        lane == 0, reward, jnp.where(lane == 1, reward * reward, jnp.where(lane == 2, length, 0.0))
    )
    stat_own[0] = stat
    statz[z * 2 + core] = stat

    pl.semaphore_wait(barrier, len(column) + NY - 1)

    zcopies = []
    for i, (d, e) in enumerate(column):
        zcopies.append(
            remote(
                kvblk.at[core ^ e], zrecv.at[z * 2 + core], zs_sem.at[i],
                zr_sem.at[d * 2 + e], peer(d, e),
            )
        )
        zcopies[-1].start()
    scopies = []
    for i, (d, e) in enumerate(column):
        scopies.append(
            remote(
                stat_own.at[0], statz.at[z * 2 + core], ss_sem.at[i], sr_sem.at[d * 2 + e], peer(d, e)
            )
        )
        scopies[-1].start()
    partner = device(y, z, other)
    xcopies = [
        remote(q_hbm.at[:, pl.ds(other_q, 1024)], q_in.at[core], xs_sem.at[0], xr_sem.at[0], partner),
        remote(do_hbm.at[:, pl.ds(other_q, 1024)], do_in.at[core], xs_sem.at[1], xr_sem.at[1], partner),
        remote(
            rkv_hbm.at[:, :, pl.ds(other_kv, 256)], rkv_in.at[core], xs_sem.at[2], xr_sem.at[2], partner
        ),
    ]
    for copy in xcopies:
        copy.start()

    ycopies = []
    for d in range(NZ):
        for e in range(2):
            if d or e:
                slot = (z ^ d) * 2 + (core ^ e)
                remote(
                    kvblk.at[0], zrecv.at[slot], zs_sem.at[0], zr_sem.at[d * 2 + e], peer(d, e)
                ).wait_recv()
        zz = z ^ d
        first = zrecv[zz * 2].astype(F32)
        second = zrecv[zz * 2 + 1].astype(F32)
        at = pl.ds(pl.multiple_of(y * (NZ * 16) + zz * 16, 16), 16)
        kv_all[0, at, :] = jnp.concatenate([first[:8], second[:8]], axis=0).astype(BF16)
        kv_all[1, at, :] = jnp.concatenate([first[8:], second[8:]], axis=0).astype(BF16)
        for k in range(1, NY):
            copy = remote(
                kv_all.at[:, at, :], kv_all.at[:, at, :], ys_sem.at[d * (NY - 1) + k - 1],
                yr_sem.at[k - 1], device((y + k) % NY, z, core),
            )
            copy.start()
            ycopies.append(copy)

    for i, (d, e) in enumerate(column):
        slot = (z ^ d) * 2 + (core ^ e)
        remote(
            stat_own.at[0], statz.at[slot], ss_sem.at[0], sr_sem.at[d * 2 + e], peer(d, e)
        ).wait_recv()
    column_sum = jnp.sum(statz[...], axis=0)
    staty_own[0] = column_sum
    staty[y] = column_sum
    sycopies = []
    for k in range(1, NY):
        copy = remote(
            staty_own.at[0], staty.at[y], sys_sem.at[k - 1], syr_sem.at[k - 1],
            device((y + k) % NY, z, core),
        )
        copy.start()
        sycopies.append(copy)

    for load in loads:
        load.wait()
    for copy in xcopies:
        copy.wait_recv()

    for hd in range(2):
        for j in range(2):
            for g in range(GROUP):
                col = hd * 512 + g * HD
                qcat[hd, 2 * j + g // 2, (g % 2) * ROWS : (g % 2 + 1) * ROWS, :] = q_in[
                    j, :, col : col + HD
                ]

    for k in range(1, NY):
        yy = (y + NY - k) % NY
        remote(
            staty_own.at[0], staty.at[yy], sys_sem.at[0], syr_sem.at[k - 1], device(yy, z, core)
        ).wait_recv()
    totals = jnp.sum(staty[...], axis=0)
    rollouts = float(2 * NY * NZ)
    mean = totals[:, 0:1] / rollouts
    var = totals[:, 1:2] / rollouts - mean * mean
    divisor = jnp.sqrt(var) + 1.0
    norm = float(2 * NY * NZ * ROWS) / totals[:, 2:3]
    row = lax.broadcasted_iota(jnp.int32, (ROWS, HD), 0).astype(F32)
    for j in range(2):
        own = statz[z * 2 + j]
        weight = (own[:, 0:1] - mean) / divisor * norm
        live = row < own[:, 2:3]
        for hd in range(2):
            for g in range(GROUP):
                col = hd * 512 + g * HD
                seed = do_in[j, :, col : col + HD].astype(F32)
                docat[hd, 2 * j + g // 2, (g % 2) * ROWS : (g % 2 + 1) * ROWS, :] = jnp.where(
                    live, weight * seed, 0.0
                ).astype(BF16)

    for k in range(1, NY):
        yy = (y + NY - k) % NY
        at = pl.ds(pl.multiple_of(yy * (NZ * 16), NZ * 16), NZ * 16)
        remote(
            kv_all.at[:, at, :], kv_all.at[:, at, :], ys_sem.at[0], yr_sem.at[k - 1], device(yy, z, core)
        ).wait_recv()

    def strips(hd):
        cols = slice(hd * HD, (hd + 1) * HD)

        def strip(s, carry):
            j = s // 2
            q = qcat[hd, s]
            do = docat[hd, s]
            kp = kv_all[0, :, cols]
            vp = kv_all[1, :, cols]
            ko = rkv_in[j, 0, :, cols]
            vo = rkv_in[j, 1, :, cols]
            key = lax.broadcasted_iota(jnp.int32, (ROWS, 256), 0)
            query = lax.broadcasted_iota(jnp.int32, (ROWS, 256), 1) % ROWS
            sp = dot(kp, q, NT)
            so = jnp.where(key <= query, dot(ko, q, NT), -1e30)
            top = jnp.maximum(
                jnp.max(sp, axis=0, keepdims=True), jnp.max(so, axis=0, keepdims=True)
            )
            ep = jnp.exp2((sp - top) * (SCALE * LOG2E))
            eo = jnp.exp2((so - top) * (SCALE * LOG2E))
            total = jnp.sum(ep, axis=0, keepdims=True) + jnp.sum(eo, axis=0, keepdims=True)
            inverse = 1.0 / total
            dp = dot(vp, do, NT)
            dn = dot(vo, do, NT)
            row_dot = (
                jnp.sum(ep * dp, axis=0, keepdims=True) + jnp.sum(eo * dn, axis=0, keepdims=True)
            ) * inverse
            pp = ep * inverse
            po = eo * inverse
            at = pl.ds(pl.multiple_of(s * 256, 256), 256)
            p_sc[:prefix, at] = pp.astype(BF16)
            p_sc[prefix:, at] = po.astype(BF16)
            ds_sc[:prefix, at] = (pp * (dp - row_dot)).astype(BF16)
            ds_sc[prefix:, at] = (po * (dn - row_dot)).astype(BF16)
            return carry

        lax.fori_loop(0, 4, strip, 0)

    rycopies = []

    def prefix_grads(hd):
        qs = qcat[hd].reshape(1024, HD)
        dos = docat[hd].reshape(1024, HD)
        for k in range(1, NY + 1):
            yy = (y + k) % NY
            at = pl.ds(pl.multiple_of(yy * (NZ * 16), NZ * 16), NZ * 16)
            gk = dot(ds_sc[at, :], qs) * SCALE
            gv = dot(p_sc[at, :], dos)
            if k == NY:
                yown[hd, 0] = gk
                yown[hd, 1] = gv
            else:
                ysend[hd, k - 1, 0] = gk.astype(BF16)
                ysend[hd, k - 1, 1] = gv.astype(BF16)
                copy = remote(
                    ysend.at[hd, k - 1], yrecv.at[hd, k - 1], rys_sem.at[hd, k - 1],
                    ryr_sem.at[hd, k - 1], device(yy, z, core),
                )
                copy.start()
                rycopies.append(copy)

    def local_grads(hd):
        cols = slice(hd * HD, (hd + 1) * HD)
        for j in range(2):
            qs = qcat[hd, 2 * j : 2 * j + 2].reshape(512, HD)
            dos = docat[hd, 2 * j : 2 * j + 2].reshape(512, HD)
            at = slice(j * 512, j * 512 + 512)
            grkv_st[j, 0, :, cols] = (dot(ds_sc[prefix:, at], qs) * SCALE).astype(BF16)
            grkv_st[j, 1, :, cols] = dot(p_sc[prefix:, at], dos).astype(BF16)

        def query_strip(s, carry):
            j = s // 2
            at = pl.ds(pl.multiple_of(s * 256, 256), 256)
            kp = kv_all[0, :, cols]
            ko = rkv_in[j, 0, :, cols]
            grad = dot(kp, ds_sc[:prefix, at], TN) + dot(ko, ds_sc[prefix:, at], TN)
            grad = (grad * SCALE).T.astype(BF16)
            for g in range(2):
                col = pl.multiple_of(hd * 512 + (s % 2) * 256 + g * HD, HD)
                gq_st[j, :, pl.ds(col, HD)] = grad[g * ROWS : (g + 1) * ROWS]
            return carry

        lax.fori_loop(0, 4, query_strip, 0)

    rzcopies = []

    def row_sums(hd):
        for k in range(1, NY):
            remote(
                ysend.at[hd, k - 1], yrecv.at[hd, k - 1], rys_sem.at[hd, k - 1],
                ryr_sem.at[hd, k - 1], device((y + NY - k) % NY, z, core),
            ).wait_recv()
        sums = [
            yown[hd, i]
            + (yrecv[hd, 0, i].astype(F32) + yrecv[hd, 1, i].astype(F32) + yrecv[hd, 2, i].astype(F32))
            for i in range(2)
        ]
        for zz in range(NZ):
            for cc in range(2):
                at = slice(zz * 16 + cc * 8, zz * 16 + cc * 8 + 8)
                zsend[hd, zz * 2 + cc] = jnp.concatenate([sums[0][at], sums[1][at]], axis=0).astype(BF16)
        zback[hd, z * 2 + core] = zsend[hd, z * 2 + core]
        for i, (d, e) in enumerate(column):
            copy = remote(
                zsend.at[hd, (z ^ d) * 2 + (core ^ e)], zback.at[hd, z * 2 + core],
                rzs_sem.at[hd, i], rzr_sem.at[hd, d * 2 + e], peer(d, e),
            )
            copy.start()
            rzcopies.append(copy)

    strips(0)
    prefix_grads(0)
    local_grads(0)
    strips(1)
    prefix_grads(1)
    row_sums(0)
    local_grads(1)
    outs = [
        pltpu.make_async_copy(gq_st.at[core], gq_hbm.at[:, pl.ds(my_q, 1024)], out_sem.at[0]),
        pltpu.make_async_copy(grkv_st.at[core], grkv_hbm.at[:, :, pl.ds(my_kv, 256)], out_sem.at[1]),
    ]
    ocopies = [
        remote(gq_st.at[other], gq_hbm.at[:, pl.ds(my_q, 1024)], os_sem.at[0], or_sem.at[0], partner),
        remote(
            grkv_st.at[other], grkv_hbm.at[:, :, pl.ds(my_kv, 256)], os_sem.at[1], or_sem.at[1], partner
        ),
    ]
    for copy in ocopies + outs:
        copy.start()
    row_sums(1)

    for hd in range(2):
        for d, e in column:
            slot = (z ^ d) * 2 + (core ^ e)
            remote(
                zsend.at[hd, slot], zback.at[hd, slot], rzs_sem.at[hd, 0],
                rzr_sem.at[hd, d * 2 + e], peer(d, e),
            ).wait_recv()
    for cc in range(2):
        for hd in range(2):
            total = zback[hd, cc].astype(F32)
            for zz in range(1, NZ):
                total = total + zback[hd, zz * 2 + cc].astype(F32)
            cols = slice(cc * 256 + hd * HD, cc * 256 + (hd + 1) * HD)
            gp_ref[0, :, cols] = total[:8]
            gp_ref[1, :, cols] = total[8:]

    for copy in outs:
        copy.wait()
    for copy in ocopies:
        copy.wait()
    for copy in zcopies + scopies + xcopies + ycopies + sycopies + rycopies + rzcopies:
        copy.wait_send()


def local(queries, roll_kv, prefix_kv, grad_seed, lengths, rewards):
    prefix = NY * NZ * 16
    keys = prefix + ROWS
    near = NZ * 16
    vmem = pltpu.VMEM
    sem = pltpu.SemaphoreType.DMA
    anywhere = pl.BlockSpec(memory_space=pl.ANY)
    whole = pl.BlockSpec(memory_space=pltpu.VMEM)
    scalar = pl.BlockSpec(memory_space=pltpu.SMEM)
    ncol = 2 * NZ
    gq, grkv, gp = pl.pallas_call(
        kernel,
        out_shape=(
            jax.ShapeDtypeStruct(queries.shape, BF16),
            jax.ShapeDtypeStruct(roll_kv.shape, BF16),
            jax.ShapeDtypeStruct((2, 8, 512), F32),
        ),
        in_specs=[anywhere, anywhere, whole, anywhere, scalar, scalar],
        out_specs=(anywhere, anywhere, whole),
        scratch_shapes=[
            vmem((2, 16, 256), BF16),
            vmem((ncol, 16, 256), BF16),
            vmem((2, prefix, 256), BF16),
            vmem((1, 1, 128), F32),
            vmem((ncol, 1, 128), F32),
            vmem((1, 1, 128), F32),
            vmem((NY, 1, 128), F32),
            vmem((2, ROWS, 1024), BF16),
            vmem((2, ROWS, 1024), BF16),
            vmem((2, 2, ROWS, 256), BF16),
            vmem((2, 4, 256, HD), BF16),
            vmem((2, 4, 256, HD), BF16),
            vmem((keys, 1024), BF16),
            vmem((keys, 1024), BF16),
            vmem((2, NY - 1, 2, near, HD), BF16),
            vmem((2, NY - 1, 2, near, HD), BF16),
            vmem((2, 2, near, HD), F32),
            vmem((2, ncol, 16, HD), BF16),
            vmem((2, ncol, 16, HD), BF16),
            vmem((2, ROWS, 1024), BF16),
            vmem((2, 2, ROWS, 256), BF16),
            sem((ncol,)), sem((ncol,)),
            sem((ncol,)), sem((ncol,)),
            sem((NZ * (NY - 1),)), sem((NY - 1,)),
            sem((NY - 1,)), sem((NY - 1,)),
            sem((3,)), sem((3,)), sem((3,)),
            sem((2, NY - 1)), sem((2, NY - 1)),
            sem((2, ncol)), sem((2, ncol)),
            sem((2,)), sem((2,)), sem((2,)),
        ],
        compiler_params=pltpu.CompilerParams(
            collective_id=0, has_side_effects=True, vmem_limit_bytes=40 * 2**20
        ),
        name="prefix_attention_backward",
    )(queries, roll_kv, prefix_kv, grad_seed, lengths, rewards)
    return gq, grkv, gp.transpose(1, 0, 2).astype(BF16)


def solution(mesh):
    rows = ("group", "rollout")
    return jax.shard_map(
        local,
        mesh=mesh,
        in_specs=(
            P(rows, None), P(None, rows, None), P(rows, None, None), P(rows, None), P(rows), P(rows),
        ),
        out_specs=(P(rows, None), P(None, rows, None), P(rows, None, None)),
        check_vma=False,
    )
```

```python
import functools
import math

import jax
import jax.numpy as jnp
from jax import lax
from jax.experimental import pallas as pl
from jax.experimental.pallas import tpu as pltpu
from jax.sharding import PartitionSpec as P

HD = 128
GROUP = 4
NY = 4
NZ = 8
ROWS = 128
SCALE = 1.0 / math.sqrt(HD)
LOG2E = 1.4426950408889634
UNROLL = 4
MESH = pl.DeviceIdType.MESH
F32 = jnp.float32
BF16 = jnp.bfloat16
NT = (((1,), (1,)), ((), ()))
TN = (((0,), (0,)), ((), ()))


def dot(a, b, dims=(((1,), (0,)), ((), ()))):
    return lax.dot_general(a, b, dims, preferred_element_type=F32)


def kernel(
    q_hbm, rkv_hbm, pkv_hbm, do_hbm, len_hbm, rew_hbm,
    gq_ref, grkv_ref, gp_ref,
    gp_st, pkv_in, len_in, rew_in, kvblk, zrecv, kv_all, stat_own, statz, staty_own, staty,
    q_in, do_in, rkv_in, qcat, docat, e_sc, dp_sc, top_sc, sum_sc, dot_sc, p_sc, ds_sc, weights,
    ysend, yrecv, yown, zsend, zback, gq_st, grkv_st, gq_back, grkv_back,
    zs_sem, zr_sem, ss_sem, sr_sem, ys_sem, yr_sem, sys_sem, syr_sem,
    in_sem, xs_sem, xr_sem, rys_sem, ryr_sem, rzs_sem, rzr_sem, out_sem, os_sem, or_sem,
):
    group = lax.axis_index("group")
    index = lax.axis_index("rollout")
    y = index // (2 * NZ)
    z = (index // 2) % NZ
    core = index % 2
    other = 1 - core
    prefix = NY * NZ * 16

    def device(yy, zz, cc):
        return (group, (yy * NZ + zz) * 2 + cc)

    def remote(src, dst, ssem, rsem, where):
        return pltpu.make_async_remote_copy(
            src_ref=src, dst_ref=dst, send_sem=ssem, recv_sem=rsem,
            device_id=where, device_id_type=MESH,
        )

    column = [(d, e) for d in range(NZ) for e in range(2) if d or e]

    def peer(d, e):
        return device(y, z ^ d, core ^ e)

    barrier = pltpu.get_barrier_semaphore()
    for d, e in column:
        pl.semaphore_signal(barrier, inc=1, device_id=peer(d, e), device_id_type=MESH)
    for d in range(1, NY):
        pl.semaphore_signal(
            barrier, inc=1, device_id=device((y + d) % NY, z, core), device_id_type=MESH
        )

    my_q = pl.multiple_of(core * 1024, 1024)
    other_q = pl.multiple_of(other * 1024, 1024)
    my_kv = pl.multiple_of(core * 256, 256)
    other_kv = pl.multiple_of(other * 256, 256)
    loads = [
        pltpu.make_async_copy(q_hbm.at[:, pl.ds(my_q, 1024)], q_in.at[core], in_sem.at[0]),
        pltpu.make_async_copy(do_hbm.at[:, pl.ds(my_q, 1024)], do_in.at[core], in_sem.at[1]),
        pltpu.make_async_copy(rkv_hbm.at[:, :, pl.ds(my_kv, 256)], rkv_in.at[core], in_sem.at[2]),
    ]
    small = [
        pltpu.make_async_copy(pkv_hbm, pkv_in, in_sem.at[3]),
        pltpu.make_async_copy(len_hbm, len_in, in_sem.at[4]),
        pltpu.make_async_copy(rew_hbm, rew_in, in_sem.at[5]),
    ]
    for load in small + loads:
        load.start()
    for load in small:
        load.wait()

    pair = pkv_in[...].astype(F32)
    own_k = pair[:, 0, :]
    own_v = pair[:, 1, :]
    for hd in range(2):
        for cc in range(2):
            cols = slice(cc * 256 + hd * HD, cc * 256 + hd * HD + HD)
            kvblk[hd, cc] = jnp.concatenate([own_k[:, cols], own_v[:, cols]], axis=0).astype(BF16)
        zrecv[hd, z * 2 + core] = kvblk[hd, core]

    lane = lax.broadcasted_iota(jnp.int32, (1, 128), 1)
    reward = rew_in[0].astype(F32)
    length = len_in[0].astype(F32)
    stat = jnp.where(
        lane == 0, reward, jnp.where(lane == 1, reward * reward, jnp.where(lane == 2, length, 0.0))
    )
    stat_own[0] = stat
    statz[z * 2 + core] = stat

    pl.semaphore_wait(barrier, len(column) + NY - 1)

    zcopies = []

    def column_send(hd):
        for i, (d, e) in enumerate(column):
            zcopies.append(
                remote(
                    kvblk.at[hd, core ^ e], zrecv.at[hd, z * 2 + core], zs_sem.at[hd, i],
                    zr_sem.at[hd, d * 2 + e], peer(d, e),
                )
            )
            zcopies[-1].start()

    column_send(0)
    scopies = []
    for i, (d, e) in enumerate(column):
        scopies.append(
            remote(
                stat_own.at[0], statz.at[z * 2 + core], ss_sem.at[i], sr_sem.at[d * 2 + e], peer(d, e)
            )
        )
        scopies[-1].start()
    column_send(1)
    partner = device(y, z, other)
    xcopies = [
        remote(q_hbm.at[:, pl.ds(other_q, 1024)], q_in.at[core], xs_sem.at[0], xr_sem.at[0], partner),
        remote(
            rkv_hbm.at[:, :, pl.ds(other_kv, 256)], rkv_in.at[core], xs_sem.at[1], xr_sem.at[1], partner
        ),
        remote(do_hbm.at[:, pl.ds(other_q, 1024)], do_in.at[core], xs_sem.at[2], xr_sem.at[2], partner),
    ]
    for copy in xcopies:
        copy.start()

    ycopies = []

    def row_send(hd):
        for d in range(NZ):
            for e in range(2):
                if d or e:
                    slot = (z ^ d) * 2 + (core ^ e)
                    remote(
                        kvblk.at[hd, 0], zrecv.at[hd, slot], zs_sem.at[hd, 0], zr_sem.at[hd, d * 2 + e],
                        peer(d, e),
                    ).wait_recv()
            zz = z ^ d
            first = zrecv[hd, zz * 2].astype(F32)
            second = zrecv[hd, zz * 2 + 1].astype(F32)
            at = pl.ds(pl.multiple_of(zz * 16, 16), 16)
            kv_all[hd, 0, 0, at, :] = jnp.concatenate([first[:8], second[:8]], axis=0).astype(BF16)
            kv_all[hd, 1, 0, at, :] = jnp.concatenate([first[8:], second[8:]], axis=0).astype(BF16)
            for k in range(1, NY):
                copy = remote(
                    kv_all.at[hd, :, 0, at, :], kv_all.at[hd, :, k, at, :],
                    ys_sem.at[hd, d * (NY - 1) + k - 1], yr_sem.at[hd, k - 1],
                    device((y + k) % NY, z, core),
                )
                copy.start()
                ycopies.append(copy)

    def block(hd, slot):
        cols = slice(hd * HD, (hd + 1) * HD)

        def strip(s, carry):
            if slot == NY:
                k_rows = rkv_in[s // 2, 0, :, cols]
                v_rows = rkv_in[s // 2, 1, :, cols]
            else:
                k_rows = kv_all[hd, 0, slot]
                v_rows = kv_all[hd, 1, slot]
            scores = dot(k_rows, qcat[hd, s], NT)
            if slot == NY:
                key = lax.broadcasted_iota(jnp.int32, (ROWS, 256), 0)
                query = lax.broadcasted_iota(jnp.int32, (ROWS, 256), 1) % ROWS
                scores = jnp.where(key <= query, scores, -1e30)
            grad_soft = dot(v_rows, docat[hd, s], NT)
            top = jnp.max(scores, axis=0, keepdims=True)
            powers = jnp.exp2((scores - top) * (SCALE * LOG2E))
            e_sc[hd, s, slot] = powers
            dp_sc[hd, s, slot] = grad_soft
            top_sc[hd, s, slot] = top
            sum_sc[hd, s, slot] = jnp.sum(powers, axis=0, keepdims=True)
            dot_sc[hd, s, slot] = jnp.sum(powers * grad_soft, axis=0, keepdims=True)
            return carry

        lax.fori_loop(0, 4, strip, 0, unroll=UNROLL)

    for load in loads:
        load.wait()
    for copy in xcopies:
        copy.wait_recv()
    for hd in range(2):
        for j in range(2):
            for g in range(GROUP):
                col = hd * 512 + g * HD
                at = slice((g % 2) * ROWS, (g % 2 + 1) * ROWS)
                qcat[hd, 2 * j + g // 2, at, :] = q_in[j, :, col : col + HD]
                docat[hd, 2 * j + g // 2, at, :] = do_in[j, :, col : col + HD]
    block(0, NY)
    block(1, NY)
    row_send(0)
    for i, (d, e) in enumerate(column):
        slot = (z ^ d) * 2 + (core ^ e)
        remote(
            stat_own.at[0], statz.at[slot], ss_sem.at[0], sr_sem.at[d * 2 + e], peer(d, e)
        ).wait_recv()
    column_sum = jnp.sum(statz[...], axis=0)
    staty_own[0] = column_sum
    staty[y] = column_sum
    sycopies = []
    for k in range(1, NY):
        copy = remote(
            staty_own.at[0], staty.at[y], sys_sem.at[k - 1], syr_sem.at[k - 1],
            device((y + k) % NY, z, core),
        )
        copy.start()
        sycopies.append(copy)

    row_send(1)
    block(0, 0)
    block(1, 0)

    def row_wait(hd, k):
        remote(
            kv_all.at[hd, :, 0], kv_all.at[hd, :, k], ys_sem.at[hd, 0], yr_sem.at[hd, k - 1],
            device((y + NY - k) % NY, z, core),
        ).wait_recv()

    for k in (1, 3, 2):
        row_wait(0, k)
        block(0, k)

    for k in range(1, NY):
        yy = (y + NY - k) % NY
        remote(
            staty_own.at[0], staty.at[yy], sys_sem.at[0], syr_sem.at[k - 1], device(yy, z, core)
        ).wait_recv()
    totals = jnp.sum(staty[...], axis=0)
    rollouts = float(2 * NY * NZ)
    mean = totals[:, 0:1] / rollouts
    var = totals[:, 1:2] / rollouts - mean * mean
    divisor = jnp.sqrt(var) + 1.0
    norm = float(2 * NY * NZ * ROWS) / totals[:, 2:3]
    step = (lax.broadcasted_iota(jnp.int32, (1, 256), 1) % ROWS).astype(F32)
    for j in range(2):
        own = statz[z * 2 + j]
        weight = (own[:, 0:1] - mean) / divisor * norm
        weights[j] = jnp.where(step < own[:, 2:3], weight, 0.0)

    def finish(hd):
        def strip(s, carry):
            tops = [top_sc[hd, s, b] for b in range(NY + 1)]
            top = functools.reduce(jnp.maximum, tops)
            factors = [jnp.exp2((t - top) * (SCALE * LOG2E)) for t in tops]
            total = sum(sum_sc[hd, s, b] * factors[b] for b in range(NY + 1))
            inverse = 1.0 / total
            row_dot = sum(dot_sc[hd, s, b] * factors[b] for b in range(NY + 1)) * inverse
            scaled = weights[s // 2] * inverse
            at = pl.ds(pl.multiple_of(s * 256, 256), 256)
            for b in range(NY + 1):
                soft = e_sc[hd, s, b] * (factors[b] * scaled)
                rows = slice(b * ROWS, (b + 1) * ROWS)
                p_sc[hd, rows, at] = soft.astype(BF16)
                ds_sc[hd, rows, at] = (soft * (dp_sc[hd, s, b] - row_dot)).astype(BF16)
            return carry

        lax.fori_loop(0, 4, strip, 0, unroll=4)

    rycopies = []

    def prefix_grads(hd, kind):
        held, rows = (ds_sc, qcat) if kind == 0 else (p_sc, docat)
        grad = dot(held[hd, :prefix, :], rows[hd].reshape(1024, HD))
        if kind == 0:
            grad = grad * SCALE
        yown[hd, kind] = grad[:ROWS]
        for k in range(1, NY):
            ysend[hd, kind, k - 1] = grad[k * ROWS : (k + 1) * ROWS].astype(BF16)
            copy = remote(
                ysend.at[hd, kind, k - 1], yrecv.at[hd, kind, k - 1], rys_sem.at[hd, kind, k - 1],
                ryr_sem.at[hd, kind, k - 1], device((y + NY - k) % NY, z, core),
            )
            copy.start()
            rycopies.append(copy)

    def local_grads(hd):
        cols = slice(hd * HD, (hd + 1) * HD)
        for j in range(2):
            qs = qcat[hd, 2 * j : 2 * j + 2].reshape(512, HD)
            dos = docat[hd, 2 * j : 2 * j + 2].reshape(512, HD)
            at = slice(j * 512, j * 512 + 512)
            grkv_st[j, 0, :, cols] = (dot(ds_sc[hd, prefix:, at], qs) * SCALE).astype(BF16)
            grkv_st[j, 1, :, cols] = dot(p_sc[hd, prefix:, at], dos).astype(BF16)

        def query_strip(s, carry):
            j = s // 2
            at = pl.ds(pl.multiple_of(s * 256, 256), 256)
            kp = kv_all[hd, 0].reshape(prefix, HD)
            ko = rkv_in[j, 0, :, cols]
            grad = dot(kp, ds_sc[hd, :prefix, at], TN) + dot(ko, ds_sc[hd, prefix:, at], TN)
            grad = (grad * SCALE).T.astype(BF16)
            for g in range(2):
                col = pl.multiple_of(hd * 512 + (s % 2) * 256 + g * HD, HD)
                gq_st[j, :, pl.ds(col, HD)] = grad[g * ROWS : (g + 1) * ROWS]
            return carry

        lax.fori_loop(0, 4, query_strip, 0, unroll=UNROLL)

    rzcopies = []

    def row_sums(hd):
        for k in range(1, NY):
            for kind in range(2):
                remote(
                    ysend.at[hd, kind, k - 1], yrecv.at[hd, kind, k - 1], rys_sem.at[hd, kind, k - 1],
                    ryr_sem.at[hd, kind, k - 1], device((y + k) % NY, z, core),
                ).wait_recv()
        sums = [
            yown[hd, i]
            + (yrecv[hd, i, 0].astype(F32) + yrecv[hd, i, 1].astype(F32) + yrecv[hd, i, 2].astype(F32))
            for i in range(2)
        ]
        for zz in range(NZ):
            for cc in range(2):
                at = slice(zz * 16 + cc * 8, zz * 16 + cc * 8 + 8)
                zsend[hd, zz * 2 + cc] = jnp.concatenate([sums[0][at], sums[1][at]], axis=0).astype(BF16)
        zback[hd, z * 2 + core] = zsend[hd, z * 2 + core]
        for i, (d, e) in enumerate(column):
            copy = remote(
                zsend.at[hd, (z ^ d) * 2 + (core ^ e)], zback.at[hd, z * 2 + core],
                rzs_sem.at[hd, i], rzr_sem.at[hd, d * 2 + e], peer(d, e),
            )
            copy.start()
            rzcopies.append(copy)

    for hd in range(2):
        if hd == 1:
            for k in (1, 3, 2):
                row_wait(1, k)
                block(1, k)
        finish(hd)
        prefix_grads(hd, 1)
        prefix_grads(hd, 0)
    row_sums(0)
    local_grads(0)
    local_grads(1)
    outs = [
        pltpu.make_async_copy(gq_st.at[core], gq_ref.at[:, pl.ds(my_q, 1024)], out_sem.at[0]),
        pltpu.make_async_copy(grkv_st.at[core], grkv_ref.at[:, :, pl.ds(my_kv, 256)], out_sem.at[1]),
    ]
    ocopies = [
        remote(gq_st.at[other], gq_back, os_sem.at[0], or_sem.at[0], partner),
        remote(grkv_st.at[other], grkv_back, os_sem.at[1], or_sem.at[1], partner),
    ]
    for copy in ocopies + outs:
        copy.start()
    row_sums(1)
    backs = [
        pltpu.make_async_copy(gq_back, gq_ref.at[:, pl.ds(other_q, 1024)], out_sem.at[3]),
        pltpu.make_async_copy(grkv_back, grkv_ref.at[:, :, pl.ds(other_kv, 256)], out_sem.at[4]),
    ]
    for copy, back in zip(ocopies, backs):
        copy.wait_recv()
        back.start()
    outs = outs + backs

    for hd in range(2):
        for d, e in column:
            slot = (z ^ d) * 2 + (core ^ e)
            remote(
                zsend.at[hd, slot], zback.at[hd, slot], rzs_sem.at[hd, 0],
                rzr_sem.at[hd, d * 2 + e], peer(d, e),
            ).wait_recv()
    for cc in range(2):
        for hd in range(2):
            total = zback[hd, cc].astype(F32)
            for zz in range(1, NZ):
                total = total + zback[hd, zz * 2 + cc].astype(F32)
            cols = slice(cc * 256 + hd * HD, cc * 256 + (hd + 1) * HD)
            gp_st[0, :, cols] = total[:8]
            gp_st[1, :, cols] = total[8:]
    outs.append(pltpu.make_async_copy(gp_st, gp_ref, out_sem.at[2]))
    outs[-1].start()

    for copy in outs:
        copy.wait()
    for copy in ocopies + zcopies + scopies + xcopies + ycopies + sycopies + rycopies + rzcopies:
        copy.wait_send()


def emit(gq_from, grkv_from, gp_from, gq_to, grkv_to, gp_to, sums, pairs, gq, grkv, fetch_sem, put_sem):
    ways = [(gp_from, sums, None), (grkv_from, grkv, grkv_to)]
    for i in range(4):
        at = pl.ds(i * 32, 32)
        ways.append((gq_from.at[at], gq.at[at], gq_to.at[at]))
    fetches = [pltpu.make_async_copy(way[0], way[1], fetch_sem.at[i]) for i, way in enumerate(ways)]
    for fetch in fetches:
        fetch.start()
    fetches[0].wait()
    pairs[...] = jnp.stack([sums[0], sums[1]], axis=1).astype(BF16)
    puts = [pltpu.make_async_copy(pairs, gp_to, put_sem.at[0])]
    puts[0].start()
    for i in range(1, len(ways)):
        fetches[i].wait()
        puts.append(pltpu.make_async_copy(ways[i][1], ways[i][2], put_sem.at[i]))
        puts[i].start()
    for put in puts:
        put.wait()


def local(queries, roll_kv, prefix_kv, grad_seed, lengths, rewards):
    prefix = NY * NZ * 16
    keys = prefix + ROWS
    near = NZ * 16
    vmem = pltpu.VMEM
    sem = pltpu.SemaphoreType.DMA
    hbm = pl.BlockSpec(memory_space=pltpu.HBM)
    ncol = 2 * NZ
    grads = pl.pallas_call(
        kernel,
        out_shape=(
            jax.ShapeDtypeStruct(queries.shape, BF16),
            jax.ShapeDtypeStruct(roll_kv.shape, BF16),
            jax.ShapeDtypeStruct((2, 8, 512), F32),
        ),
        in_specs=[hbm] * 6,
        out_specs=(hbm, hbm, hbm),
        scratch_shapes=[
            vmem((2, 8, 512), F32),
            vmem(prefix_kv.shape, BF16),
            pltpu.SMEM((1,), jnp.int32),
            pltpu.SMEM((1,), jnp.int32),
            vmem((2, 2, 16, HD), BF16),
            vmem((2, ncol, 16, HD), BF16),
            vmem((2, 2, NY, near, HD), BF16),
            vmem((1, 1, 128), F32),
            vmem((ncol, 1, 128), F32),
            vmem((1, 1, 128), F32),
            vmem((NY, 1, 128), F32),
            vmem((2, ROWS, 1024), BF16),
            vmem((2, ROWS, 1024), BF16),
            vmem((2, 2, ROWS, 256), BF16),
            vmem((2, 4, 256, HD), BF16),
            vmem((2, 4, 256, HD), BF16),
            vmem((2, 4, NY + 1, ROWS, 256), F32),
            vmem((2, 4, NY + 1, ROWS, 256), F32),
            vmem((2, 4, NY + 1, 1, 256), F32),
            vmem((2, 4, NY + 1, 1, 256), F32),
            vmem((2, 4, NY + 1, 1, 256), F32),
            vmem((2, keys, 1024), BF16),
            vmem((2, keys, 1024), BF16),
            vmem((2, 1, 256), F32),
            vmem((2, 2, NY - 1, near, HD), BF16),
            vmem((2, 2, NY - 1, near, HD), BF16),
            vmem((2, 2, near, HD), F32),
            vmem((2, ncol, 16, HD), BF16),
            vmem((2, ncol, 16, HD), BF16),
            vmem((2, ROWS, 1024), BF16),
            vmem((2, 2, ROWS, 256), BF16),
            vmem((ROWS, 1024), BF16),
            vmem((2, ROWS, 256), BF16),
            sem((2, ncol)), sem((2, ncol)),
            sem((ncol,)), sem((ncol,)),
            sem((2, NZ * (NY - 1))), sem((2, NY - 1)),
            sem((NY - 1,)), sem((NY - 1,)),
            sem((6,)), sem((3,)), sem((3,)),
            sem((2, 2, NY - 1)), sem((2, 2, NY - 1)),
            sem((2, ncol)), sem((2, ncol)),
            sem((5,)), sem((2,)), sem((2,)),
        ],
        compiler_params=pltpu.CompilerParams(
            collective_id=0, has_side_effects=True, vmem_limit_bytes=60 * 2**20
        ),
        name="prefix_attention_backward",
    )(queries, roll_kv, prefix_kv, grad_seed, lengths, rewards)
    return pl.pallas_call(
        emit,
        out_shape=(
            jax.ShapeDtypeStruct(queries.shape, BF16),
            jax.ShapeDtypeStruct(roll_kv.shape, BF16),
            jax.ShapeDtypeStruct(prefix_kv.shape, BF16),
        ),
        in_specs=[hbm] * 3,
        out_specs=[hbm] * 3,
        scratch_shapes=[
            vmem((2, 8, 512), F32), vmem(prefix_kv.shape, BF16), vmem(queries.shape, BF16),
            vmem(roll_kv.shape, BF16), sem((6,)), sem((6,)),
        ],
        compiler_params=pltpu.CompilerParams(vmem_limit_bytes=60 * 2**20),
        name="emit",
    )(*grads)


def solution(mesh):
    rows = ("group", "rollout")
    return jax.shard_map(
        local,
        mesh=mesh,
        in_specs=(
            P(rows, None), P(None, rows, None), P(rows, None, None), P(rows, None), P(rows), P(rows),
        ),
        out_specs=(P(rows, None), P(None, rows, None), P(rows, None, None)),
        check_vma=False,
    )
```

```python
import functools
import math

import jax
import jax.numpy as jnp
from jax import lax
from jax.experimental import pallas as pl
from jax.experimental.pallas import tpu as pltpu
from jax.sharding import PartitionSpec as P

HD = 128
GROUP = 4
NY = 4
NZ = 8
ROWS = 128
SCALE = 1.0 / math.sqrt(HD)
LOG2E = 1.4426950408889634
UNROLL = 4
MESH = pl.DeviceIdType.MESH
F32 = jnp.float32
BF16 = jnp.bfloat16
NT = (((1,), (1,)), ((), ()))
TN = (((0,), (0,)), ((), ()))


def dot(a, b, dims=(((1,), (0,)), ((), ()))):
    return lax.dot_general(a, b, dims, preferred_element_type=F32)


def kernel(
    q_hbm, rkv_hbm, pkv_hbm, do_hbm, len_hbm, rew_hbm,
    gq_ref, grkv_ref, gp_ref,
    gp_st, pkv_in, len_in, rew_in, kvblk, zrecv, kv_all, stat_own, statz, staty_own, staty,
    q_in, do_in, rkv_in, qcat, docat, e_sc, dp_sc, top_sc, sum_sc, dot_sc, p_sc, ds_sc, weights,
    ysend, yrecv, yown, zsend, zback, gq_st, grkv_st, gq_back, grkv_back,
    zs_sem, zr_sem, ss_sem, sr_sem, ys_sem, yr_sem, sys_sem, syr_sem,
    in_sem, xs_sem, xr_sem, rys_sem, ryr_sem, rzs_sem, rzr_sem, out_sem, os_sem, or_sem,
):
    group = lax.axis_index("group")
    index = lax.axis_index("rollout")
    y = index // (2 * NZ)
    z = (index // 2) % NZ
    core = index % 2
    other = 1 - core
    prefix = NY * NZ * 16

    def device(yy, zz, cc):
        return (group, (yy * NZ + zz) * 2 + cc)

    def remote(src, dst, ssem, rsem, where):
        return pltpu.make_async_remote_copy(
            src_ref=src, dst_ref=dst, send_sem=ssem, recv_sem=rsem,
            device_id=where, device_id_type=MESH,
        )

    column = [(d, e) for d in reversed(range(NZ)) for e in range(2) if d or e]

    def peer(d, e):
        return device(y, z ^ d, core ^ e)

    barrier = pltpu.get_barrier_semaphore()
    for d, e in column:
        pl.semaphore_signal(barrier, inc=1, device_id=peer(d, e), device_id_type=MESH)
    for d in range(1, NY):
        pl.semaphore_signal(
            barrier, inc=1, device_id=device((y + d) % NY, z, core), device_id_type=MESH
        )

    my_q = pl.multiple_of(core * 1024, 1024)
    other_q = pl.multiple_of(other * 1024, 1024)
    my_kv = pl.multiple_of(core * 256, 256)
    other_kv = pl.multiple_of(other * 256, 256)
    loads = [
        pltpu.make_async_copy(q_hbm.at[:, pl.ds(my_q, 1024)], q_in.at[core], in_sem.at[0]),
        pltpu.make_async_copy(do_hbm.at[:, pl.ds(my_q, 1024)], do_in.at[core], in_sem.at[1]),
        pltpu.make_async_copy(rkv_hbm.at[:, :, pl.ds(my_kv, 256)], rkv_in.at[core], in_sem.at[2]),
    ]
    small = [
        pltpu.make_async_copy(pkv_hbm, pkv_in, in_sem.at[3]),
        pltpu.make_async_copy(len_hbm, len_in, in_sem.at[4]),
        pltpu.make_async_copy(rew_hbm, rew_in, in_sem.at[5]),
    ]
    for load in small + loads:
        load.start()
    for load in small:
        load.wait()

    pair = pkv_in[...].astype(F32)
    own_k = pair[:, 0, :]
    own_v = pair[:, 1, :]
    for hd in range(2):
        for cc in range(2):
            cols = slice(cc * 256 + hd * HD, cc * 256 + hd * HD + HD)
            kvblk[hd, cc] = jnp.concatenate([own_k[:, cols], own_v[:, cols]], axis=0).astype(BF16)
        zrecv[hd, z * 2 + core] = kvblk[hd, core]

    lane = lax.broadcasted_iota(jnp.int32, (1, 128), 1)
    reward = rew_in[0].astype(F32)
    length = len_in[0].astype(F32)
    stat = jnp.where(
        lane == 0, reward, jnp.where(lane == 1, reward * reward, jnp.where(lane == 2, length, 0.0))
    )
    stat_own[0] = stat
    statz[z * 2 + core] = stat

    pl.semaphore_wait(barrier, len(column) + NY - 1)

    def column_send(hd):
        for d, e in column:
            remote(
                kvblk.at[hd, core ^ e], zrecv.at[hd, z * 2 + core], zs_sem.at[0], zr_sem.at[hd, d],
                peer(d, e),
            ).start()

    column_send(0)
    for d, e in column:
        remote(stat_own.at[0], statz.at[z * 2 + core], ss_sem.at[0], sr_sem.at[0], peer(d, e)).start()
    column_send(1)
    partner = device(y, z, other)
    xcopies = [
        remote(q_hbm.at[:, pl.ds(other_q, 1024)], q_in.at[core], xs_sem.at[0], xr_sem.at[0], partner),
        remote(
            rkv_hbm.at[:, :, pl.ds(other_kv, 256)], rkv_in.at[core], xs_sem.at[1], xr_sem.at[1], partner
        ),
        remote(do_hbm.at[:, pl.ds(other_q, 1024)], do_in.at[core], xs_sem.at[2], xr_sem.at[2], partner),
    ]
    for copy in xcopies:
        copy.start()

    def row_send(hd):
        for d in range(NZ):
            zz = z ^ d
            landed = zrecv.at[hd, pl.ds(zz * 2, 2)] if d else zrecv.at[hd, pl.ds(z * 2 + other, 1)]
            remote(landed, landed, zs_sem.at[0], zr_sem.at[hd, d], peer(d or 1, 0)).wait_recv()
            first = zrecv[hd, zz * 2].astype(F32)
            second = zrecv[hd, zz * 2 + 1].astype(F32)
            at = pl.ds(pl.multiple_of(zz * 16, 16), 16)
            kv_all[hd, 0, 0, at, :] = jnp.concatenate([first[:8], second[:8]], axis=0).astype(BF16)
            kv_all[hd, 1, 0, at, :] = jnp.concatenate([first[8:], second[8:]], axis=0).astype(BF16)
            for k in (2, 1, 3):
                remote(
                    kv_all.at[hd, :, 0, at, :], kv_all.at[hd, :, k, at, :], ys_sem.at[0],
                    yr_sem.at[hd, k - 1], device((y + k) % NY, z, core),
                ).start()

    def block(hd, slot):
        cols = slice(hd * HD, (hd + 1) * HD)

        def strip(s, carry):
            if slot == NY:
                k_rows = rkv_in[s // 2, 0, :, cols]
                v_rows = rkv_in[s // 2, 1, :, cols]
            else:
                k_rows = kv_all[hd, 0, slot]
                v_rows = kv_all[hd, 1, slot]
            scores = dot(k_rows, qcat[hd, s], NT)
            if slot == NY:
                key = lax.broadcasted_iota(jnp.int32, (ROWS, 256), 0)
                query = lax.broadcasted_iota(jnp.int32, (ROWS, 256), 1) % ROWS
                scores = jnp.where(key <= query, scores, -1e30)
            grad_soft = dot(v_rows, docat[hd, s], NT)
            top = jnp.max(scores, axis=0, keepdims=True)
            powers = jnp.exp2((scores - top) * (SCALE * LOG2E))
            e_sc[hd, s, slot] = powers
            dp_sc[hd, s, slot] = grad_soft
            top_sc[hd, s, slot] = top
            sum_sc[hd, s, slot] = jnp.sum(powers, axis=0, keepdims=True)
            dot_sc[hd, s, slot] = jnp.sum(powers * grad_soft, axis=0, keepdims=True)
            return carry

        lax.fori_loop(0, 4, strip, 0, unroll=UNROLL)

    for load in loads:
        load.wait()
    for copy in xcopies:
        copy.wait_recv()
    for hd in range(2):
        for j in range(2):
            for g in range(GROUP):
                col = hd * 512 + g * HD
                at = slice((g % 2) * ROWS, (g % 2 + 1) * ROWS)
                qcat[hd, 2 * j + g // 2, at, :] = q_in[j, :, col : col + HD]
                docat[hd, 2 * j + g // 2, at, :] = do_in[j, :, col : col + HD]
    block(0, NY)
    block(1, NY)
    row_send(0)
    all_but_one = statz.at[pl.ds(0, len(column))]
    stats = remote(all_but_one, all_but_one, ss_sem.at[0], sr_sem.at[0], peer(1, 0))
    stats.wait_recv()
    column_sum = jnp.sum(statz[...], axis=0)
    staty_own[0] = column_sum
    staty[y] = column_sum
    for k in range(1, NY):
        remote(
            staty_own.at[0], staty.at[y], sys_sem.at[0], syr_sem.at[0], device((y + k) % NY, z, core)
        ).start()

    row_send(1)
    block(0, 0)
    block(1, 0)

    def row_wait(hd, k):
        remote(
            kv_all.at[hd, :, 0], kv_all.at[hd, :, k], ys_sem.at[0], yr_sem.at[hd, k - 1],
            device((y + NY - k) % NY, z, core),
        ).wait_recv()

    for k in (1, 3, 2):
        row_wait(0, k)
        block(0, k)

    next_row = device((y + 1) % NY, z, core)
    other_rows = staty.at[pl.ds(0, NY - 1)]
    row_stats = remote(other_rows, other_rows, sys_sem.at[0], syr_sem.at[0], next_row)
    row_stats.wait_recv()
    totals = jnp.sum(staty[...], axis=0)
    rollouts = float(2 * NY * NZ)
    mean = totals[:, 0:1] / rollouts
    var = totals[:, 1:2] / rollouts - mean * mean
    divisor = jnp.sqrt(var) + 1.0
    norm = float(2 * NY * NZ * ROWS) / totals[:, 2:3]
    step = (lax.broadcasted_iota(jnp.int32, (1, 256), 1) % ROWS).astype(F32)
    for j in range(2):
        own = statz[z * 2 + j]
        weight = (own[:, 0:1] - mean) / divisor * norm
        weights[j] = jnp.where(step < own[:, 2:3], weight, 0.0)

    def finish(hd):
        def strip(s, carry):
            tops = [top_sc[hd, s, b] for b in range(NY + 1)]
            top = functools.reduce(jnp.maximum, tops)
            factors = [jnp.exp2((t - top) * (SCALE * LOG2E)) for t in tops]
            total = sum(sum_sc[hd, s, b] * factors[b] for b in range(NY + 1))
            inverse = 1.0 / total
            row_dot = sum(dot_sc[hd, s, b] * factors[b] for b in range(NY + 1)) * inverse
            scaled = weights[s // 2] * inverse
            at = pl.ds(pl.multiple_of(s * 256, 256), 256)
            for b in range(NY + 1):
                soft = e_sc[hd, s, b] * (factors[b] * scaled)
                rows = slice(b * ROWS, (b + 1) * ROWS)
                p_sc[hd, rows, at] = soft.astype(BF16)
                ds_sc[hd, rows, at] = (soft * (dp_sc[hd, s, b] - row_dot)).astype(BF16)
            return carry

        lax.fori_loop(0, 4, strip, 0, unroll=4)

    def prefix_grads(hd, kind):
        held, rows = (ds_sc, qcat) if kind == 0 else (p_sc, docat)
        grad = dot(held[hd, :prefix, :], rows[hd].reshape(1024, HD))
        if kind == 0:
            grad = grad * SCALE
        yown[hd, kind] = grad[:ROWS]
        for k in (2, 1, 3):
            ysend[hd, kind, k - 1] = grad[k * ROWS : (k + 1) * ROWS].astype(BF16)
            remote(
                ysend.at[hd, kind, k - 1], yrecv.at[hd, kind, k - 1], rys_sem.at[0], ryr_sem.at[hd],
                device((y + NY - k) % NY, z, core),
            ).start()

    def local_grads(hd):
        cols = slice(hd * HD, (hd + 1) * HD)
        for j in range(2):
            qs = qcat[hd, 2 * j : 2 * j + 2].reshape(512, HD)
            dos = docat[hd, 2 * j : 2 * j + 2].reshape(512, HD)
            at = slice(j * 512, j * 512 + 512)
            grkv_st[j, 0, :, cols] = (dot(ds_sc[hd, prefix:, at], qs) * SCALE).astype(BF16)
            grkv_st[j, 1, :, cols] = dot(p_sc[hd, prefix:, at], dos).astype(BF16)

        def query_strip(s, carry):
            j = s // 2
            at = pl.ds(pl.multiple_of(s * 256, 256), 256)
            kp = kv_all[hd, 0].reshape(prefix, HD)
            ko = rkv_in[j, 0, :, cols]
            grad = dot(kp, ds_sc[hd, :prefix, at], TN) + dot(ko, ds_sc[hd, prefix:, at], TN)
            grad = (grad * SCALE).T.astype(BF16)
            for g in range(2):
                col = pl.multiple_of(hd * 512 + (s % 2) * 256 + g * HD, HD)
                gq_st[j, :, pl.ds(col, HD)] = grad[g * ROWS : (g + 1) * ROWS]
            return carry

        lax.fori_loop(0, 4, query_strip, 0, unroll=UNROLL)

    def row_sums(hd):
        remote(ysend.at[hd], yrecv.at[hd], rys_sem.at[0], ryr_sem.at[hd], next_row).wait_recv()
        sums = [
            yown[hd, i]
            + (yrecv[hd, i, 0].astype(F32) + yrecv[hd, i, 1].astype(F32) + yrecv[hd, i, 2].astype(F32))
            for i in range(2)
        ]
        for zz in range(NZ):
            for cc in range(2):
                at = slice(zz * 16 + cc * 8, zz * 16 + cc * 8 + 8)
                zsend[hd, zz * 2 + cc] = jnp.concatenate([sums[0][at], sums[1][at]], axis=0).astype(BF16)
        zback[hd, z * 2 + core] = zsend[hd, z * 2 + core]
        for d, e in column:
            remote(
                zsend.at[hd, (z ^ d) * 2 + (core ^ e)], zback.at[hd, z * 2 + core], rzs_sem.at[0],
                rzr_sem.at[hd], peer(d, e),
            ).start()

    for hd in range(2):
        if hd == 1:
            for k in (1, 3, 2):
                row_wait(1, k)
                block(1, k)
        finish(hd)
        prefix_grads(hd, 1)
        prefix_grads(hd, 0)
    local_grads(0)
    local_grads(1)
    outs = [
        pltpu.make_async_copy(gq_st.at[core], gq_ref.at[:, pl.ds(my_q, 1024)], out_sem.at[0]),
        pltpu.make_async_copy(grkv_st.at[core], grkv_ref.at[:, :, pl.ds(my_kv, 256)], out_sem.at[1]),
    ]
    ocopies = [
        remote(gq_st.at[other], gq_back, os_sem.at[0], or_sem.at[0], partner),
        remote(grkv_st.at[other], grkv_back, os_sem.at[1], or_sem.at[1], partner),
    ]
    for copy in ocopies + outs:
        copy.start()
    row_sums(0)
    row_sums(1)
    backs = [
        pltpu.make_async_copy(gq_back, gq_ref.at[:, pl.ds(other_q, 1024)], out_sem.at[3]),
        pltpu.make_async_copy(grkv_back, grkv_ref.at[:, :, pl.ds(other_kv, 256)], out_sem.at[4]),
    ]
    for copy, back in zip(ocopies, backs):
        copy.wait_recv()
        back.start()
    outs = outs + backs

    for hd in range(2):
        landed = zback.at[hd, pl.ds(0, len(column))]
        remote(landed, landed, rzs_sem.at[0], rzr_sem.at[hd], peer(1, 0)).wait_recv()
    for cc in range(2):
        for hd in range(2):
            total = zback[hd, cc].astype(F32)
            for zz in range(1, NZ):
                total = total + zback[hd, zz * 2 + cc].astype(F32)
            cols = slice(cc * 256 + hd * HD, cc * 256 + (hd + 1) * HD)
            gp_st[0, :, cols] = total[:8]
            gp_st[1, :, cols] = total[8:]
    outs.append(pltpu.make_async_copy(gp_st, gp_ref, out_sem.at[2]))
    outs[-1].start()

    for copy in outs:
        copy.wait()
    for copy in ocopies + xcopies:
        copy.wait_send()
    stats.wait_send()
    row_stats.wait_send()
    for held, sem in (
        (zrecv.at[:, pl.ds(0, len(column))], zs_sem.at[0]),
        (kv_all.at[:, :, pl.ds(1, NY - 1)], ys_sem.at[0]),
        (ysend, rys_sem.at[0]),
        (zsend.at[:, pl.ds(0, len(column))], rzs_sem.at[0]),
    ):
        remote(held, held, sem, sem, next_row).wait_send()


def emit(gq_from, grkv_from, gp_from, gq_to, grkv_to, gp_to, sums, pairs, gq, grkv, fetch_sem, put_sem):
    ways = [(gp_from, sums, None), (grkv_from, grkv, grkv_to)]
    for i in range(4):
        at = pl.ds(i * 32, 32)
        ways.append((gq_from.at[at], gq.at[at], gq_to.at[at]))
    fetches = [pltpu.make_async_copy(way[0], way[1], fetch_sem.at[i]) for i, way in enumerate(ways)]
    for fetch in fetches:
        fetch.start()
    fetches[0].wait()
    pairs[...] = jnp.stack([sums[0], sums[1]], axis=1).astype(BF16)
    puts = [pltpu.make_async_copy(pairs, gp_to, put_sem.at[0])]
    puts[0].start()
    for i in range(1, len(ways)):
        fetches[i].wait()
        puts.append(pltpu.make_async_copy(ways[i][1], ways[i][2], put_sem.at[i]))
        puts[i].start()
    for put in puts:
        put.wait()


def local(queries, roll_kv, prefix_kv, grad_seed, lengths, rewards):
    prefix = NY * NZ * 16
    keys = prefix + ROWS
    near = NZ * 16
    vmem = pltpu.VMEM
    sem = pltpu.SemaphoreType.DMA
    hbm = pl.BlockSpec(memory_space=pltpu.HBM)
    ncol = 2 * NZ
    grads = pl.pallas_call(
        kernel,
        out_shape=(
            jax.ShapeDtypeStruct(queries.shape, BF16),
            jax.ShapeDtypeStruct(roll_kv.shape, BF16),
            jax.ShapeDtypeStruct((2, 8, 512), F32),
        ),
        in_specs=[hbm] * 6,
        out_specs=(hbm, hbm, hbm),
        scratch_shapes=[
            vmem((2, 8, 512), F32),
            vmem(prefix_kv.shape, BF16),
            pltpu.SMEM((1,), jnp.int32),
            pltpu.SMEM((1,), jnp.int32),
            vmem((2, 2, 16, HD), BF16),
            vmem((2, ncol, 16, HD), BF16),
            vmem((2, 2, NY, near, HD), BF16),
            vmem((1, 1, 128), F32),
            vmem((ncol, 1, 128), F32),
            vmem((1, 1, 128), F32),
            vmem((NY, 1, 128), F32),
            vmem((2, ROWS, 1024), BF16),
            vmem((2, ROWS, 1024), BF16),
            vmem((2, 2, ROWS, 256), BF16),
            vmem((2, 4, 256, HD), BF16),
            vmem((2, 4, 256, HD), BF16),
            vmem((2, 4, NY + 1, ROWS, 256), F32),
            vmem((2, 4, NY + 1, ROWS, 256), F32),
            vmem((2, 4, NY + 1, 1, 256), F32),
            vmem((2, 4, NY + 1, 1, 256), F32),
            vmem((2, 4, NY + 1, 1, 256), F32),
            vmem((2, keys, 1024), BF16),
            vmem((2, keys, 1024), BF16),
            vmem((2, 1, 256), F32),
            vmem((2, 2, NY - 1, near, HD), BF16),
            vmem((2, 2, NY - 1, near, HD), BF16),
            vmem((2, 2, near, HD), F32),
            vmem((2, ncol, 16, HD), BF16),
            vmem((2, ncol, 16, HD), BF16),
            vmem((2, ROWS, 1024), BF16),
            vmem((2, 2, ROWS, 256), BF16),
            vmem((ROWS, 1024), BF16),
            vmem((2, ROWS, 256), BF16),
            sem((1,)), sem((2, NZ)),
            sem((1,)), sem((1,)),
            sem((1,)), sem((2, NY - 1)),
            sem((1,)), sem((1,)),
            sem((6,)), sem((3,)), sem((3,)),
            sem((1,)), sem((2,)),
            sem((1,)), sem((2,)),
            sem((5,)), sem((2,)), sem((2,)),
        ],
        compiler_params=pltpu.CompilerParams(
            collective_id=0, has_side_effects=True, vmem_limit_bytes=60 * 2**20
        ),
        name="prefix_attention_backward",
    )(queries, roll_kv, prefix_kv, grad_seed, lengths, rewards)
    return pl.pallas_call(
        emit,
        out_shape=(
            jax.ShapeDtypeStruct(queries.shape, BF16),
            jax.ShapeDtypeStruct(roll_kv.shape, BF16),
            jax.ShapeDtypeStruct(prefix_kv.shape, BF16),
        ),
        in_specs=[hbm] * 3,
        out_specs=[hbm] * 3,
        scratch_shapes=[
            vmem((2, 8, 512), F32), vmem(prefix_kv.shape, BF16), vmem(queries.shape, BF16),
            vmem(roll_kv.shape, BF16), sem((6,)), sem((6,)),
        ],
        compiler_params=pltpu.CompilerParams(vmem_limit_bytes=60 * 2**20),
        name="emit",
    )(*grads)


def solution(mesh):
    rows = ("group", "rollout")
    return jax.shard_map(
        local,
        mesh=mesh,
        in_specs=(
            P(rows, None), P(None, rows, None), P(rows, None, None), P(rows, None), P(rows), P(rows),
        ),
        out_specs=(P(rows, None), P(None, rows, None), P(rows, None, None)),
        check_vma=False,
    )
```

```python
import functools
import math

import jax
import jax.numpy as jnp
from jax import lax
from jax.experimental import pallas as pl
from jax.experimental.pallas import tpu as pltpu
from jax.sharding import PartitionSpec as P

HD = 128
GROUP = 4
NY = 4
NZ = 8
ROWS = 128
SCALE = 1.0 / math.sqrt(HD)
LOG2E = 1.4426950408889634
UNROLL = 4
MESH = pl.DeviceIdType.MESH
F32 = jnp.float32
BF16 = jnp.bfloat16
NT = (((1,), (1,)), ((), ()))
TN = (((0,), (0,)), ((), ()))


def dot(a, b, dims=(((1,), (0,)), ((), ()))):
    return lax.dot_general(a, b, dims, preferred_element_type=F32)


def kernel(
    q_hbm, rkv_hbm, pkv_hbm, do_hbm, len_hbm, rew_hbm,
    gq_ref, grkv_ref, zback,
    pkv_in, len_in, rew_in, kvblk, zrecv, kv_all, stat_own, statz, staty_own, staty,
    q_in, do_in, rkv_in, qcat, docat, e_sc, dp_sc, top_sc, sum_sc, dot_sc, p_sc, ds_sc, weights,
    ysend, yrecv, yown, zsend, gq_st, grkv_st, gq_back, grkv_back,
    zs_sem, zr_sem, ss_sem, sr_sem, ys_sem, yr_sem, sys_sem, syr_sem,
    in_sem, xs_sem, xr_sem, rys_sem, ryr_sem, rzs_sem, rzr_sem, out_sem, os_sem, or_sem,
):
    group = lax.axis_index("group")
    index = lax.axis_index("rollout")
    y = index // (2 * NZ)
    z = (index // 2) % NZ
    core = index % 2
    other = 1 - core
    prefix = NY * NZ * 16

    def device(yy, zz, cc):
        return (group, (yy * NZ + zz) * 2 + cc)

    def remote(src, dst, ssem, rsem, where):
        return pltpu.make_async_remote_copy(
            src_ref=src, dst_ref=dst, send_sem=ssem, recv_sem=rsem,
            device_id=where, device_id_type=MESH,
        )

    column = [(d, e) for d in reversed(range(NZ)) for e in range(2) if d or e]
    half = NZ // 2
    close = [(d, e) for d, e in column if d <= half]

    def peer(d, e):
        return device(y, z ^ d, core ^ e)

    barrier = pltpu.get_barrier_semaphore()
    for d, e in close:
        pl.semaphore_signal(barrier, inc=1, device_id=peer(d, e), device_id_type=MESH)
    for d in range(1, NY):
        pl.semaphore_signal(
            barrier, inc=1, device_id=device((y + d) % NY, z, core), device_id_type=MESH
        )

    my_q = pl.multiple_of(core * 1024, 1024)
    other_q = pl.multiple_of(other * 1024, 1024)
    my_kv = pl.multiple_of(core * 256, 256)
    other_kv = pl.multiple_of(other * 256, 256)
    loads = [
        pltpu.make_async_copy(q_hbm.at[:, pl.ds(my_q, 1024)], q_in.at[core], in_sem.at[0]),
        pltpu.make_async_copy(do_hbm.at[:, pl.ds(my_q, 1024)], do_in.at[core], in_sem.at[1]),
        pltpu.make_async_copy(rkv_hbm.at[:, :, pl.ds(my_kv, 256)], rkv_in.at[core], in_sem.at[2]),
    ]
    small = [
        pltpu.make_async_copy(pkv_hbm, pkv_in, in_sem.at[3]),
        pltpu.make_async_copy(len_hbm, len_in, in_sem.at[4]),
        pltpu.make_async_copy(rew_hbm, rew_in, in_sem.at[5]),
    ]
    for load in small + loads:
        load.start()
    for load in small:
        load.wait()

    pair = pkv_in[...].astype(F32)
    own_k = pair[:, 0, :]
    own_v = pair[:, 1, :]
    for hd in range(2):
        for cc in range(2):
            cols = slice(cc * 256 + hd * HD, cc * 256 + hd * HD + HD)
            kvblk[hd, cc] = jnp.concatenate([own_k[:, cols], own_v[:, cols]], axis=0).astype(BF16)
        zrecv[hd, z * 2 + core] = kvblk[hd, core]

    lane = lax.broadcasted_iota(jnp.int32, (1, 128), 1)
    reward = rew_in[0].astype(F32)
    length = len_in[0].astype(F32)
    stat = jnp.where(
        lane == 0, reward, jnp.where(lane == 1, reward * reward, jnp.where(lane == 2, length, 0.0))
    )
    stat_own[0] = stat
    statz[z * 2 + core] = stat

    pl.semaphore_wait(barrier, len(close) + NY - 1)

    def column_send(hd):
        for d, e in close:
            remote(
                kvblk.at[hd, core ^ e], zrecv.at[hd, z * 2 + core], zs_sem.at[0], zr_sem.at[hd, d],
                peer(d, e),
            ).start()

    column_send(0)
    for d, e in close:
        remote(
            stat_own.at[0], statz.at[z * 2 + core], ss_sem.at[0], sr_sem.at[d // half], peer(d, e)
        ).start()
    column_send(1)
    partner = device(y, z, other)
    xcopies = [
        remote(q_hbm.at[:, pl.ds(other_q, 1024)], q_in.at[core], xs_sem.at[0], xr_sem.at[0], partner),
        remote(
            rkv_hbm.at[:, :, pl.ds(other_kv, 256)], rkv_in.at[core], xs_sem.at[1], xr_sem.at[1], partner
        ),
        remote(do_hbm.at[:, pl.ds(other_q, 1024)], do_in.at[core], xs_sem.at[2], xr_sem.at[2], partner),
    ]
    for copy in xcopies:
        copy.start()

    def row_send(hd):
        for d in range(NZ):
            zz = z ^ d
            landed = zrecv.at[hd, pl.ds(zz * 2, 2)] if d else zrecv.at[hd, pl.ds(z * 2 + other, 1)]
            if d != half:
                remote(landed, landed, zs_sem.at[0], zr_sem.at[hd, d], peer(d or 1, 0)).wait_recv()
            first = zrecv[hd, zz * 2].astype(F32)
            second = zrecv[hd, zz * 2 + 1].astype(F32)
            at = pl.ds(pl.multiple_of(zz * 16, 16), 16)
            kv_all[hd, 0, 0, at, :] = jnp.concatenate([first[:8], second[:8]], axis=0).astype(BF16)
            kv_all[hd, 1, 0, at, :] = jnp.concatenate([first[8:], second[8:]], axis=0).astype(BF16)
            for k in (2, 1, 3):
                remote(
                    kv_all.at[hd, :, 0, at, :], kv_all.at[hd, :, k, at, :], ys_sem.at[0],
                    yr_sem.at[hd, k - 1], device((y + k) % NY, z, core),
                ).start()

    def block(hd, slot):
        cols = slice(hd * HD, (hd + 1) * HD)

        def strip(s, carry):
            if slot == NY:
                k_rows = rkv_in[s // 2, 0, :, cols]
                v_rows = rkv_in[s // 2, 1, :, cols]
            else:
                k_rows = kv_all[hd, 0, slot]
                v_rows = kv_all[hd, 1, slot]
            scores = dot(k_rows, qcat[hd, s], NT)
            if slot == NY:
                key = lax.broadcasted_iota(jnp.int32, (ROWS, 256), 0)
                query = lax.broadcasted_iota(jnp.int32, (ROWS, 256), 1) % ROWS
                scores = jnp.where(key <= query, scores, -1e30)
            grad_soft = dot(v_rows, docat[hd, s], NT)
            top = jnp.max(scores, axis=0, keepdims=True)
            powers = jnp.exp2((scores - top) * (SCALE * LOG2E))
            e_sc[hd, s, slot] = powers
            dp_sc[hd, s, slot] = grad_soft
            top_sc[hd, s, slot] = top
            sum_sc[hd, s, slot] = jnp.sum(powers, axis=0, keepdims=True)
            dot_sc[hd, s, slot] = jnp.sum(powers * grad_soft, axis=0, keepdims=True)
            return carry

        lax.fori_loop(0, 4, strip, 0, unroll=UNROLL)

    for load in loads:
        load.wait()
    for copy in xcopies:
        copy.wait_recv()
    for hd in range(2):
        for j in range(2):
            for g in range(GROUP):
                col = hd * 512 + g * HD
                at = slice((g % 2) * ROWS, (g % 2 + 1) * ROWS)
                qcat[hd, 2 * j + g // 2, at, :] = q_in[j, :, col : col + HD]
                docat[hd, 2 * j + g // 2, at, :] = do_in[j, :, col : col + HD]
    block(0, NY)
    block(1, NY)
    mirror = pl.ds((z ^ half) * 2, 2)

    def pass_on(hd):
        block_pair = zrecv.at[hd, mirror]
        remote(block_pair, block_pair, zs_sem.at[0], zr_sem.at[hd, half], peer(half, 0)).wait_recv()
        for d in reversed(range(1, half)):
            remote(block_pair, block_pair, zs_sem.at[0], zr_sem.at[hd, half + d], peer(d, 0)).start()

    pass_on(0)
    stat_pair = statz.at[mirror]
    remote(stat_pair, stat_pair, ss_sem.at[0], sr_sem.at[1], peer(half, 0)).wait_recv()
    for d in reversed(range(1, half)):
        remote(stat_pair, stat_pair, ss_sem.at[0], sr_sem.at[0], peer(d, 0)).start()
    pass_on(1)
    row_send(0)
    all_but_one = statz.at[pl.ds(0, len(column))]
    stats = remote(all_but_one, all_but_one, ss_sem.at[0], sr_sem.at[0], peer(1, 0))
    unmirrored = statz.at[pl.ds(0, len(column) - 2)]
    remote(unmirrored, unmirrored, ss_sem.at[0], sr_sem.at[0], peer(1, 0)).wait_recv()
    column_sum = jnp.sum(statz[...], axis=0)
    staty_own[0] = column_sum
    staty[y] = column_sum
    for k in range(1, NY):
        remote(
            staty_own.at[0], staty.at[y], sys_sem.at[0], syr_sem.at[0], device((y + k) % NY, z, core)
        ).start()

    row_send(1)
    block(0, 0)
    block(1, 0)

    def row_wait(hd, k):
        remote(
            kv_all.at[hd, :, 0], kv_all.at[hd, :, k], ys_sem.at[0], yr_sem.at[hd, k - 1],
            device((y + NY - k) % NY, z, core),
        ).wait_recv()

    for k in (1, 3, 2):
        row_wait(0, k)
        block(0, k)

    next_row = device((y + 1) % NY, z, core)
    other_rows = staty.at[pl.ds(0, NY - 1)]
    row_stats = remote(other_rows, other_rows, sys_sem.at[0], syr_sem.at[0], next_row)
    row_stats.wait_recv()
    totals = jnp.sum(staty[...], axis=0)
    rollouts = float(2 * NY * NZ)
    mean = totals[:, 0:1] / rollouts
    var = totals[:, 1:2] / rollouts - mean * mean
    divisor = jnp.sqrt(var) + 1.0
    norm = float(2 * NY * NZ * ROWS) / totals[:, 2:3]
    step = (lax.broadcasted_iota(jnp.int32, (1, 256), 1) % ROWS).astype(F32)
    for j in range(2):
        own = statz[z * 2 + j]
        weight = (own[:, 0:1] - mean) / divisor * norm
        weights[j] = jnp.where(step < own[:, 2:3], weight, 0.0)

    def finish(hd):
        def strip(s, carry):
            tops = [top_sc[hd, s, b] for b in range(NY + 1)]
            top = functools.reduce(jnp.maximum, tops)
            factors = [jnp.exp2((t - top) * (SCALE * LOG2E)) for t in tops]
            total = sum(sum_sc[hd, s, b] * factors[b] for b in range(NY + 1))
            inverse = 1.0 / total
            row_dot = sum(dot_sc[hd, s, b] * factors[b] for b in range(NY + 1)) * inverse
            scaled = weights[s // 2] * inverse
            at = pl.ds(pl.multiple_of(s * 256, 256), 256)
            for b in range(NY + 1):
                soft = e_sc[hd, s, b] * (factors[b] * scaled)
                rows = slice(b * ROWS, (b + 1) * ROWS)
                p_sc[hd, rows, at] = soft.astype(BF16)
                ds_sc[hd, rows, at] = (soft * (dp_sc[hd, s, b] - row_dot)).astype(BF16)
            return carry

        lax.fori_loop(0, 4, strip, 0, unroll=4)

    def prefix_grads(hd, kind):
        held, rows = (ds_sc, qcat) if kind == 0 else (p_sc, docat)
        grad = dot(held[hd, :prefix, :], rows[hd].reshape(1024, HD))
        if kind == 0:
            grad = grad * SCALE
        yown[hd, kind] = grad[:ROWS]
        for k in (2, 1, 3):
            ysend[hd, kind, k - 1] = grad[k * ROWS : (k + 1) * ROWS].astype(BF16)
            remote(
                ysend.at[hd, kind, k - 1], yrecv.at[hd, kind, k - 1], rys_sem.at[0], ryr_sem.at[hd],
                device((y + NY - k) % NY, z, core),
            ).start()

    def local_grads(hd):
        cols = slice(hd * HD, (hd + 1) * HD)
        for j in range(2):
            qs = qcat[hd, 2 * j : 2 * j + 2].reshape(512, HD)
            dos = docat[hd, 2 * j : 2 * j + 2].reshape(512, HD)
            at = slice(j * 512, j * 512 + 512)
            grkv_st[j, 0, :, cols] = (dot(ds_sc[hd, prefix:, at], qs) * SCALE).astype(BF16)
            grkv_st[j, 1, :, cols] = dot(p_sc[hd, prefix:, at], dos).astype(BF16)

        def query_strip(s, carry):
            j = s // 2
            at = pl.ds(pl.multiple_of(s * 256, 256), 256)
            kp = kv_all[hd, 0].reshape(prefix, HD)
            ko = rkv_in[j, 0, :, cols]
            grad = dot(kp, ds_sc[hd, :prefix, at], TN) + dot(ko, ds_sc[hd, prefix:, at], TN)
            grad = (grad * SCALE).T.astype(BF16)
            for g in range(2):
                col = pl.multiple_of(hd * 512 + (s % 2) * 256 + g * HD, HD)
                gq_st[j, :, pl.ds(col, HD)] = grad[g * ROWS : (g + 1) * ROWS]
            return carry

        lax.fori_loop(0, 4, query_strip, 0, unroll=UNROLL)

    def row_sums(hd):
        remote(ysend.at[hd], yrecv.at[hd], rys_sem.at[0], ryr_sem.at[hd], next_row).wait_recv()
        sums = [
            yown[hd, i]
            + (yrecv[hd, i, 0].astype(F32) + yrecv[hd, i, 1].astype(F32) + yrecv[hd, i, 2].astype(F32))
            for i in range(2)
        ]
        for zz in range(NZ):
            for cc in range(2):
                at = slice(zz * 16 + cc * 8, zz * 16 + cc * 8 + 8)
                zsend[hd, zz * 2 + cc] = jnp.concatenate([sums[0][at], sums[1][at]], axis=0).astype(BF16)
        own_share = pltpu.make_async_copy(
            zsend.at[hd, z * 2 + core], zback.at[hd, z * 2 + core], out_sem.at[5 + hd]
        )
        own_share.start()
        outs.append(own_share)
        for d, e in column:
            remote(
                zsend.at[hd, (z ^ d) * 2 + (core ^ e)], zback.at[hd, z * 2 + core], rzs_sem.at[0],
                rzr_sem.at[hd], peer(d, e),
            ).start()

    for hd in range(2):
        if hd == 1:
            for k in (1, 3, 2):
                row_wait(1, k)
                block(1, k)
        finish(hd)
        prefix_grads(hd, 1)
        prefix_grads(hd, 0)
    local_grads(0)
    local_grads(1)
    outs = [
        pltpu.make_async_copy(gq_st.at[core], gq_ref.at[:, pl.ds(my_q, 1024)], out_sem.at[0]),
        pltpu.make_async_copy(grkv_st.at[core], grkv_ref.at[:, :, pl.ds(my_kv, 256)], out_sem.at[1]),
    ]
    ocopies = [
        remote(gq_st.at[other], gq_back, os_sem.at[0], or_sem.at[0], partner),
        remote(grkv_st.at[other], grkv_back, os_sem.at[1], or_sem.at[1], partner),
    ]
    for copy in ocopies + outs:
        copy.start()
    row_sums(0)
    row_sums(1)
    backs = [
        pltpu.make_async_copy(gq_back, gq_ref.at[:, pl.ds(other_q, 1024)], out_sem.at[3]),
        pltpu.make_async_copy(grkv_back, grkv_ref.at[:, :, pl.ds(other_kv, 256)], out_sem.at[4]),
    ]
    for copy, back in zip(ocopies, backs):
        copy.wait_recv()
        back.start()
    outs = outs + backs

    for hd in range(2):
        landed = zback.at[hd, pl.ds(0, len(column))]
        remote(landed, landed, rzs_sem.at[0], rzr_sem.at[hd], peer(1, 0)).wait_recv()

    for copy in outs:
        copy.wait()
    for copy in ocopies + xcopies:
        copy.wait_send()
    stats.wait_send()
    row_stats.wait_send()
    for held, sem in (
        (zrecv.at[:, pl.ds(0, len(column))], zs_sem.at[0]),
        (kv_all.at[:, :, pl.ds(1, NY - 1)], ys_sem.at[0]),
        (ysend, rys_sem.at[0]),
        (zsend.at[:, pl.ds(0, len(column))], rzs_sem.at[0]),
    ):
        remote(held, held, sem, sem, next_row).wait_send()


def emit(gq_from, grkv_from, shares_from, gq_to, grkv_to, gp_to, shares, sums, pairs, gq, grkv, fetch_sem, put_sem):
    ways = [(shares_from, shares, None), (grkv_from, grkv, grkv_to)]
    for i in range(4):
        at = pl.ds(i * 32, 32)
        ways.append((gq_from.at[at], gq.at[at], gq_to.at[at]))
    fetches = [pltpu.make_async_copy(way[0], way[1], fetch_sem.at[i]) for i, way in enumerate(ways)]
    for fetch in fetches:
        fetch.start()
    fetches[0].wait()
    for cc in range(2):
        for hd in range(2):
            total = shares[hd, cc].astype(F32)
            for zz in range(1, NZ):
                total = total + shares[hd, zz * 2 + cc].astype(F32)
            cols = slice(cc * 256 + hd * HD, cc * 256 + (hd + 1) * HD)
            sums[0, :, cols] = total[:8]
            sums[1, :, cols] = total[8:]
    pairs[...] = jnp.stack([sums[0], sums[1]], axis=1).astype(BF16)
    puts = [pltpu.make_async_copy(pairs, gp_to, put_sem.at[0])]
    puts[0].start()
    for i in range(1, len(ways)):
        fetches[i].wait()
        puts.append(pltpu.make_async_copy(ways[i][1], ways[i][2], put_sem.at[i]))
        puts[i].start()
    for put in puts:
        put.wait()


def local(queries, roll_kv, prefix_kv, grad_seed, lengths, rewards):
    prefix = NY * NZ * 16
    keys = prefix + ROWS
    near = NZ * 16
    vmem = pltpu.VMEM
    sem = pltpu.SemaphoreType.DMA
    hbm = pl.BlockSpec(memory_space=pltpu.HBM)
    ncol = 2 * NZ
    grads = pl.pallas_call(
        kernel,
        out_shape=(
            jax.ShapeDtypeStruct(queries.shape, BF16),
            jax.ShapeDtypeStruct(roll_kv.shape, BF16),
            jax.ShapeDtypeStruct((2, ncol, 16, HD), BF16),
        ),
        in_specs=[hbm] * 6,
        out_specs=(hbm, hbm, hbm),
        scratch_shapes=[
            vmem(prefix_kv.shape, BF16),
            pltpu.SMEM((1,), jnp.int32),
            pltpu.SMEM((1,), jnp.int32),
            vmem((2, 2, 16, HD), BF16),
            vmem((2, ncol, 16, HD), BF16),
            vmem((2, 2, NY, near, HD), BF16),
            vmem((1, 1, 128), F32),
            vmem((ncol, 1, 128), F32),
            vmem((1, 1, 128), F32),
            vmem((NY, 1, 128), F32),
            vmem((2, ROWS, 1024), BF16),
            vmem((2, ROWS, 1024), BF16),
            vmem((2, 2, ROWS, 256), BF16),
            vmem((2, 4, 256, HD), BF16),
            vmem((2, 4, 256, HD), BF16),
            vmem((2, 4, NY + 1, ROWS, 256), F32),
            vmem((2, 4, NY + 1, ROWS, 256), F32),
            vmem((2, 4, NY + 1, 1, 256), F32),
            vmem((2, 4, NY + 1, 1, 256), F32),
            vmem((2, 4, NY + 1, 1, 256), F32),
            vmem((2, keys, 1024), BF16),
            vmem((2, keys, 1024), BF16),
            vmem((2, 1, 256), F32),
            vmem((2, 2, NY - 1, near, HD), BF16),
            vmem((2, 2, NY - 1, near, HD), BF16),
            vmem((2, 2, near, HD), F32),
            vmem((2, ncol, 16, HD), BF16),
            vmem((2, ROWS, 1024), BF16),
            vmem((2, 2, ROWS, 256), BF16),
            vmem((ROWS, 1024), BF16),
            vmem((2, ROWS, 256), BF16),
            sem((1,)), sem((2, NZ)),
            sem((1,)), sem((2,)),
            sem((1,)), sem((2, NY - 1)),
            sem((1,)), sem((1,)),
            sem((6,)), sem((3,)), sem((3,)),
            sem((1,)), sem((2,)),
            sem((1,)), sem((2,)),
            sem((7,)), sem((2,)), sem((2,)),
        ],
        compiler_params=pltpu.CompilerParams(
            collective_id=0, has_side_effects=True, vmem_limit_bytes=60 * 2**20
        ),
        name="prefix_attention_backward",
    )(queries, roll_kv, prefix_kv, grad_seed, lengths, rewards)
    return pl.pallas_call(
        emit,
        out_shape=(
            jax.ShapeDtypeStruct(queries.shape, BF16),
            jax.ShapeDtypeStruct(roll_kv.shape, BF16),
            jax.ShapeDtypeStruct(prefix_kv.shape, BF16),
        ),
        in_specs=[hbm] * 3,
        out_specs=[hbm] * 3,
        scratch_shapes=[
            vmem((2, ncol, 16, HD), BF16), vmem((2, 8, 512), F32), vmem(prefix_kv.shape, BF16),
            vmem(queries.shape, BF16),
            vmem(roll_kv.shape, BF16), sem((6,)), sem((6,)),
        ],
        compiler_params=pltpu.CompilerParams(vmem_limit_bytes=60 * 2**20),
        name="emit",
    )(*grads)


def solution(mesh):
    rows = ("group", "rollout")
    return jax.shard_map(
        local,
        mesh=mesh,
        in_specs=(
            P(rows, None), P(None, rows, None), P(rows, None, None), P(rows, None), P(rows), P(rows),
        ),
        out_specs=(P(rows, None), P(None, rows, None), P(rows, None, None)),
        check_vma=False,
    )
```

```python
import functools
import math

import jax
import jax.numpy as jnp
from jax import lax
from jax.experimental import pallas as pl
from jax.experimental.pallas import tpu as pltpu
from jax.sharding import PartitionSpec as P

HD = 128
GROUP = 4
NY = 4
NZ = 8
ROWS = 128
SCALE = 1.0 / math.sqrt(HD)
LOG2E = 1.4426950408889634
UNROLL = 4
MESH = pl.DeviceIdType.MESH
F32 = jnp.float32
BF16 = jnp.bfloat16
NT = (((1,), (1,)), ((), ()))
TN = (((0,), (0,)), ((), ()))


def dot(a, b, dims=(((1,), (0,)), ((), ()))):
    return lax.dot_general(a, b, dims, preferred_element_type=F32)


def kernel(
    q_hbm, rkv_hbm, pkv_hbm, do_hbm, len_hbm, rew_hbm,
    gq_ref, grkv_ref, zback,
    pkv_in, len_in, rew_in, kvblk, zrecv, kv_all, stat_own, statz, staty_own, staty,
    q_in, do_in, rkv_in, qcat, docat, e_sc, dp_sc, top_sc, sum_sc, dot_sc, p_sc, ds_sc, weights,
    ysend, yrecv, yown, zsend, gq_st, grkv_st, gq_back, grkv_back,
    zs_sem, zr_sem, ss_sem, sr_sem, ys_sem, yr_sem, sys_sem, syr_sem,
    in_sem, xs_sem, xr_sem, rys_sem, ryr_sem, rzs_sem, rzr_sem, out_sem, os_sem, or_sem,
):
    group = lax.axis_index("group")
    index = lax.axis_index("rollout")
    y = index // (2 * NZ)
    z = (index // 2) % NZ
    core = index % 2
    other = 1 - core
    prefix = NY * NZ * 16

    def device(yy, zz, cc):
        return (group, (yy * NZ + zz) * 2 + cc)

    def remote(src, dst, ssem, rsem, where):
        return pltpu.make_async_remote_copy(
            src_ref=src, dst_ref=dst, send_sem=ssem, recv_sem=rsem,
            device_id=where, device_id_type=MESH,
        )

    column = [(d, e) for d in reversed(range(NZ)) for e in range(2) if d or e]
    half = NZ // 2
    close = [(d, e) for d, e in column if d <= half]

    def peer(d, e):
        return device(y, z ^ d, core ^ e)

    barrier = pltpu.get_barrier_semaphore()
    for d, e in close:
        pl.semaphore_signal(barrier, inc=1, device_id=peer(d, e), device_id_type=MESH)
    for d in range(1, NY):
        pl.semaphore_signal(
            barrier, inc=1, device_id=device((y + d) % NY, z, core), device_id_type=MESH
        )

    my_q = pl.multiple_of(core * 1024, 1024)
    other_q = pl.multiple_of(other * 1024, 1024)
    my_kv = pl.multiple_of(core * 256, 256)
    other_kv = pl.multiple_of(other * 256, 256)
    loads = [
        pltpu.make_async_copy(q_hbm.at[:, pl.ds(my_q, 1024)], q_in.at[core], in_sem.at[0]),
        pltpu.make_async_copy(do_hbm.at[:, pl.ds(my_q, 1024)], do_in.at[core], in_sem.at[1]),
        pltpu.make_async_copy(rkv_hbm.at[:, :, pl.ds(my_kv, 256)], rkv_in.at[core], in_sem.at[2]),
    ]
    small = [
        pltpu.make_async_copy(pkv_hbm, pkv_in, in_sem.at[3]),
        pltpu.make_async_copy(len_hbm, len_in, in_sem.at[4]),
        pltpu.make_async_copy(rew_hbm, rew_in, in_sem.at[5]),
    ]
    for load in small + loads:
        load.start()
    for load in small:
        load.wait()

    pair = pkv_in[...].astype(F32)
    own_k = pair[:, 0, :]
    own_v = pair[:, 1, :]
    for hd in range(2):
        for cc in range(2):
            cols = slice(cc * 256 + hd * HD, cc * 256 + hd * HD + HD)
            kvblk[hd, cc] = jnp.concatenate([own_k[:, cols], own_v[:, cols]], axis=0).astype(BF16)
        zrecv[hd, z * 2 + core] = kvblk[hd, core]

    lane = lax.broadcasted_iota(jnp.int32, (1, 128), 1)
    reward = rew_in[0].astype(F32)
    length = len_in[0].astype(F32)
    stat = jnp.where(
        lane == 0, reward, jnp.where(lane == 1, reward * reward, jnp.where(lane == 2, length, 0.0))
    )
    stat_own[0] = stat
    statz[z * 2 + core] = stat

    pl.semaphore_wait(barrier, len(close) + NY - 1)

    def column_send(hd):
        for d, e in close:
            remote(
                kvblk.at[hd, core ^ e], zrecv.at[hd, z * 2 + core], zs_sem.at[0], zr_sem.at[hd, d],
                peer(d, e),
            ).start()

    column_send(0)
    for d, e in close:
        remote(
            stat_own.at[0], statz.at[z * 2 + core], ss_sem.at[0], sr_sem.at[d // half], peer(d, e)
        ).start()
    column_send(1)
    partner = device(y, z, other)
    xcopies = [
        remote(q_hbm.at[:, pl.ds(other_q, 1024)], q_in.at[core], xs_sem.at[0], xr_sem.at[0], partner),
        remote(
            rkv_hbm.at[:, :, pl.ds(other_kv, 256)], rkv_in.at[core], xs_sem.at[1], xr_sem.at[1], partner
        ),
        remote(do_hbm.at[:, pl.ds(other_q, 1024)], do_in.at[core], xs_sem.at[2], xr_sem.at[2], partner),
    ]
    for copy in xcopies:
        copy.start()

    def row_send(hd, chips):
        for d in chips:
            zz = z ^ d
            landed = zrecv.at[hd, pl.ds(zz * 2, 2)] if d else zrecv.at[hd, pl.ds(z * 2 + other, 1)]
            if d != half:
                remote(landed, landed, zs_sem.at[0], zr_sem.at[hd, d], peer(d or 1, 0)).wait_recv()
            first = zrecv[hd, zz * 2].astype(F32)
            second = zrecv[hd, zz * 2 + 1].astype(F32)
            at = pl.ds(pl.multiple_of(zz * 16, 16), 16)
            kv_all[hd, 0, 0, at, :] = jnp.concatenate([first[:8], second[:8]], axis=0).astype(BF16)
            kv_all[hd, 1, 0, at, :] = jnp.concatenate([first[8:], second[8:]], axis=0).astype(BF16)
            for k in (2, 1, 3):
                remote(
                    kv_all.at[hd, :, 0, at, :], kv_all.at[hd, :, k, at, :], ys_sem.at[0],
                    yr_sem.at[hd, k - 1], device((y + k) % NY, z, core),
                ).start()

    def block(hd, slot):
        cols = slice(hd * HD, (hd + 1) * HD)

        def strip(s, carry):
            if slot == NY:
                k_rows = rkv_in[s // 2, 0, :, cols]
                v_rows = rkv_in[s // 2, 1, :, cols]
            else:
                k_rows = kv_all[hd, 0, slot]
                v_rows = kv_all[hd, 1, slot]
            scores = dot(k_rows, qcat[hd, s], NT)
            if slot == NY:
                key = lax.broadcasted_iota(jnp.int32, (ROWS, 256), 0)
                query = lax.broadcasted_iota(jnp.int32, (ROWS, 256), 1) % ROWS
                scores = jnp.where(key <= query, scores, -1e30)
            grad_soft = dot(v_rows, docat[hd, s], NT)
            top = jnp.max(scores, axis=0, keepdims=True)
            powers = jnp.exp2((scores - top) * (SCALE * LOG2E))
            e_sc[hd, s, slot] = powers
            dp_sc[hd, s, slot] = grad_soft
            top_sc[hd, s, slot] = top
            sum_sc[hd, s, slot] = jnp.sum(powers, axis=0, keepdims=True)
            dot_sc[hd, s, slot] = jnp.sum(powers * grad_soft, axis=0, keepdims=True)
            return carry

        lax.fori_loop(0, 4, strip, 0, unroll=UNROLL)

    for load in loads:
        load.wait()
    for copy in xcopies:
        copy.wait_recv()
    for hd in range(2):
        for j in range(2):
            for g in range(GROUP):
                col = hd * 512 + g * HD
                at = slice((g % 2) * ROWS, (g % 2 + 1) * ROWS)
                qcat[hd, 2 * j + g // 2, at, :] = q_in[j, :, col : col + HD]
                docat[hd, 2 * j + g // 2, at, :] = do_in[j, :, col : col + HD]
    block(0, NY)
    block(1, NY)
    mirror = pl.ds((z ^ half) * 2, 2)

    def pass_on(hd):
        block_pair = zrecv.at[hd, mirror]
        remote(block_pair, block_pair, zs_sem.at[0], zr_sem.at[hd, half], peer(half, 0)).wait_recv()
        for d in reversed(range(1, half)):
            remote(block_pair, block_pair, zs_sem.at[0], zr_sem.at[hd, half + d], peer(d, 0)).start()

    pass_on(0)
    stat_pair = statz.at[mirror]
    remote(stat_pair, stat_pair, ss_sem.at[0], sr_sem.at[1], peer(half, 0)).wait_recv()
    for d in reversed(range(1, half)):
        remote(stat_pair, stat_pair, ss_sem.at[0], sr_sem.at[0], peer(d, 0)).start()
    pass_on(1)
    row_send(0, range(half))
    row_send(1, range(half))
    row_send(0, range(half, NZ))
    all_but_one = statz.at[pl.ds(0, len(column))]
    stats = remote(all_but_one, all_but_one, ss_sem.at[0], sr_sem.at[0], peer(1, 0))
    unmirrored = statz.at[pl.ds(0, len(column) - 2)]
    remote(unmirrored, unmirrored, ss_sem.at[0], sr_sem.at[0], peer(1, 0)).wait_recv()
    column_sum = jnp.sum(statz[...], axis=0)
    staty_own[0] = column_sum
    staty[y] = column_sum
    for k in range(1, NY):
        remote(
            staty_own.at[0], staty.at[y], sys_sem.at[0], syr_sem.at[0], device((y + k) % NY, z, core)
        ).start()

    row_send(1, range(half, NZ))
    block(0, 0)
    block(1, 0)

    def row_wait(hd, k):
        remote(
            kv_all.at[hd, :, 0], kv_all.at[hd, :, k], ys_sem.at[0], yr_sem.at[hd, k - 1],
            device((y + NY - k) % NY, z, core),
        ).wait_recv()

    for k in (1, 3, 2):
        row_wait(0, k)
        block(0, k)

    next_row = device((y + 1) % NY, z, core)
    other_rows = staty.at[pl.ds(0, NY - 1)]
    row_stats = remote(other_rows, other_rows, sys_sem.at[0], syr_sem.at[0], next_row)
    row_stats.wait_recv()
    totals = jnp.sum(staty[...], axis=0)
    rollouts = float(2 * NY * NZ)
    mean = totals[:, 0:1] / rollouts
    var = totals[:, 1:2] / rollouts - mean * mean
    divisor = jnp.sqrt(var) + 1.0
    norm = float(2 * NY * NZ * ROWS) / totals[:, 2:3]
    step = (lax.broadcasted_iota(jnp.int32, (1, 256), 1) % ROWS).astype(F32)
    for j in range(2):
        own = statz[z * 2 + j]
        weight = (own[:, 0:1] - mean) / divisor * norm
        weights[j] = jnp.where(step < own[:, 2:3], weight, 0.0)

    def finish(hd):
        def strip(s, carry):
            tops = [top_sc[hd, s, b] for b in range(NY + 1)]
            top = functools.reduce(jnp.maximum, tops)
            factors = [jnp.exp2((t - top) * (SCALE * LOG2E)) for t in tops]
            total = sum(sum_sc[hd, s, b] * factors[b] for b in range(NY + 1))
            inverse = 1.0 / total
            row_dot = sum(dot_sc[hd, s, b] * factors[b] for b in range(NY + 1)) * inverse
            scaled = weights[s // 2] * inverse
            at = pl.ds(pl.multiple_of(s * 256, 256), 256)
            for b in range(NY + 1):
                soft = e_sc[hd, s, b] * (factors[b] * scaled)
                rows = slice(b * ROWS, (b + 1) * ROWS)
                p_sc[hd, rows, at] = soft.astype(BF16)
                ds_sc[hd, rows, at] = (soft * (dp_sc[hd, s, b] - row_dot)).astype(BF16)
            return carry

        lax.fori_loop(0, 4, strip, 0, unroll=4)

    def prefix_grads(hd, kind):
        held, rows = (ds_sc, qcat) if kind == 0 else (p_sc, docat)
        grad = dot(held[hd, :prefix, :], rows[hd].reshape(1024, HD))
        if kind == 0:
            grad = grad * SCALE
        yown[hd, kind] = grad[:ROWS]
        for k in (2, 1, 3):
            ysend[hd, kind, k - 1] = grad[k * ROWS : (k + 1) * ROWS].astype(BF16)
            remote(
                ysend.at[hd, kind, k - 1], yrecv.at[hd, kind, k - 1], rys_sem.at[0], ryr_sem.at[hd],
                device((y + NY - k) % NY, z, core),
            ).start()

    def local_grads(hd):
        cols = slice(hd * HD, (hd + 1) * HD)
        for j in range(2):
            qs = qcat[hd, 2 * j : 2 * j + 2].reshape(512, HD)
            dos = docat[hd, 2 * j : 2 * j + 2].reshape(512, HD)
            at = slice(j * 512, j * 512 + 512)
            grkv_st[j, 0, :, cols] = (dot(ds_sc[hd, prefix:, at], qs) * SCALE).astype(BF16)
            grkv_st[j, 1, :, cols] = dot(p_sc[hd, prefix:, at], dos).astype(BF16)

        def query_strip(s, carry):
            j = s // 2
            at = pl.ds(pl.multiple_of(s * 256, 256), 256)
            kp = kv_all[hd, 0].reshape(prefix, HD)
            ko = rkv_in[j, 0, :, cols]
            grad = dot(kp, ds_sc[hd, :prefix, at], TN) + dot(ko, ds_sc[hd, prefix:, at], TN)
            grad = (grad * SCALE).T.astype(BF16)
            for g in range(2):
                col = pl.multiple_of(hd * 512 + (s % 2) * 256 + g * HD, HD)
                gq_st[j, :, pl.ds(col, HD)] = grad[g * ROWS : (g + 1) * ROWS]
            return carry

        lax.fori_loop(0, 4, query_strip, 0, unroll=UNROLL)

    def row_sums(hd):
        remote(ysend.at[hd], yrecv.at[hd], rys_sem.at[0], ryr_sem.at[hd], next_row).wait_recv()
        sums = [
            yown[hd, i]
            + (yrecv[hd, i, 0].astype(F32) + yrecv[hd, i, 1].astype(F32) + yrecv[hd, i, 2].astype(F32))
            for i in range(2)
        ]
        for zz in range(NZ):
            for cc in range(2):
                at = slice(zz * 16 + cc * 8, zz * 16 + cc * 8 + 8)
                zsend[hd, zz * 2 + cc] = jnp.concatenate([sums[0][at], sums[1][at]], axis=0).astype(BF16)
        own_share = pltpu.make_async_copy(
            zsend.at[hd, z * 2 + core], zback.at[hd, z * 2 + core], out_sem.at[5 + hd]
        )
        own_share.start()
        outs.append(own_share)
        for d, e in column:
            remote(
                zsend.at[hd, (z ^ d) * 2 + (core ^ e)], zback.at[hd, z * 2 + core], rzs_sem.at[0],
                rzr_sem.at[hd], peer(d, e),
            ).start()

    for hd in range(2):
        if hd == 1:
            for k in (1, 3, 2):
                row_wait(1, k)
                block(1, k)
        finish(hd)
        prefix_grads(hd, 1)
        prefix_grads(hd, 0)
    local_grads(0)
    local_grads(1)
    outs = [
        pltpu.make_async_copy(gq_st.at[core], gq_ref.at[:, pl.ds(my_q, 1024)], out_sem.at[0]),
        pltpu.make_async_copy(grkv_st.at[core], grkv_ref.at[:, :, pl.ds(my_kv, 256)], out_sem.at[1]),
    ]
    ocopies = [
        remote(gq_st.at[other], gq_back, os_sem.at[0], or_sem.at[0], partner),
        remote(grkv_st.at[other], grkv_back, os_sem.at[1], or_sem.at[1], partner),
    ]
    for copy in ocopies + outs:
        copy.start()
    row_sums(0)
    row_sums(1)
    backs = [
        pltpu.make_async_copy(gq_back, gq_ref.at[:, pl.ds(other_q, 1024)], out_sem.at[3]),
        pltpu.make_async_copy(grkv_back, grkv_ref.at[:, :, pl.ds(other_kv, 256)], out_sem.at[4]),
    ]
    for copy, back in zip(ocopies, backs):
        copy.wait_recv()
        back.start()
    outs = outs + backs

    for hd in range(2):
        landed = zback.at[hd, pl.ds(0, len(column))]
        remote(landed, landed, rzs_sem.at[0], rzr_sem.at[hd], peer(1, 0)).wait_recv()

    for copy in outs:
        copy.wait()
    for copy in ocopies + xcopies:
        copy.wait_send()
    stats.wait_send()
    row_stats.wait_send()
    for held, sem in (
        (zrecv.at[:, pl.ds(0, len(column))], zs_sem.at[0]),
        (kv_all.at[:, :, pl.ds(1, NY - 1)], ys_sem.at[0]),
        (ysend, rys_sem.at[0]),
        (zsend.at[:, pl.ds(0, len(column))], rzs_sem.at[0]),
    ):
        remote(held, held, sem, sem, next_row).wait_send()


def emit(gq_from, grkv_from, shares_from, gq_to, grkv_to, gp_to, shares, sums, pairs, gq, grkv, fetch_sem, put_sem):
    ways = [(shares_from, shares, None), (grkv_from, grkv, grkv_to)]
    for i in range(4):
        at = pl.ds(i * 32, 32)
        ways.append((gq_from.at[at], gq.at[at], gq_to.at[at]))
    fetches = [pltpu.make_async_copy(way[0], way[1], fetch_sem.at[i]) for i, way in enumerate(ways)]
    for fetch in fetches:
        fetch.start()
    puts = []
    for i in range(1, len(ways)):
        fetches[i].wait()
        puts.append(pltpu.make_async_copy(ways[i][1], ways[i][2], put_sem.at[i]))
        puts[-1].start()
    fetches[0].wait()
    for cc in range(2):
        for hd in range(2):
            total = shares[hd, cc].astype(F32)
            for zz in range(1, NZ):
                total = total + shares[hd, zz * 2 + cc].astype(F32)
            cols = slice(cc * 256 + hd * HD, cc * 256 + (hd + 1) * HD)
            sums[0, :, cols] = total[:8]
            sums[1, :, cols] = total[8:]
    pairs[...] = jnp.stack([sums[0], sums[1]], axis=1).astype(BF16)
    puts.append(pltpu.make_async_copy(pairs, gp_to, put_sem.at[0]))
    puts[-1].start()
    for put in puts:
        put.wait()


def local(queries, roll_kv, prefix_kv, grad_seed, lengths, rewards):
    prefix = NY * NZ * 16
    keys = prefix + ROWS
    near = NZ * 16
    vmem = pltpu.VMEM
    sem = pltpu.SemaphoreType.DMA
    hbm = pl.BlockSpec(memory_space=pltpu.HBM)
    ncol = 2 * NZ
    grads = pl.pallas_call(
        kernel,
        out_shape=(
            jax.ShapeDtypeStruct(queries.shape, BF16),
            jax.ShapeDtypeStruct(roll_kv.shape, BF16),
            jax.ShapeDtypeStruct((2, ncol, 16, HD), BF16),
        ),
        in_specs=[hbm] * 6,
        out_specs=(hbm, hbm, hbm),
        scratch_shapes=[
            vmem(prefix_kv.shape, BF16),
            pltpu.SMEM((1,), jnp.int32),
            pltpu.SMEM((1,), jnp.int32),
            vmem((2, 2, 16, HD), BF16),
            vmem((2, ncol, 16, HD), BF16),
            vmem((2, 2, NY, near, HD), BF16),
            vmem((1, 1, 128), F32),
            vmem((ncol, 1, 128), F32),
            vmem((1, 1, 128), F32),
            vmem((NY, 1, 128), F32),
            vmem((2, ROWS, 1024), BF16),
            vmem((2, ROWS, 1024), BF16),
            vmem((2, 2, ROWS, 256), BF16),
            vmem((2, 4, 256, HD), BF16),
            vmem((2, 4, 256, HD), BF16),
            vmem((2, 4, NY + 1, ROWS, 256), F32),
            vmem((2, 4, NY + 1, ROWS, 256), F32),
            vmem((2, 4, NY + 1, 1, 256), F32),
            vmem((2, 4, NY + 1, 1, 256), F32),
            vmem((2, 4, NY + 1, 1, 256), F32),
            vmem((2, keys, 1024), BF16),
            vmem((2, keys, 1024), BF16),
            vmem((2, 1, 256), F32),
            vmem((2, 2, NY - 1, near, HD), BF16),
            vmem((2, 2, NY - 1, near, HD), BF16),
            vmem((2, 2, near, HD), F32),
            vmem((2, ncol, 16, HD), BF16),
            vmem((2, ROWS, 1024), BF16),
            vmem((2, 2, ROWS, 256), BF16),
            vmem((ROWS, 1024), BF16),
            vmem((2, ROWS, 256), BF16),
            sem((1,)), sem((2, NZ)),
            sem((1,)), sem((2,)),
            sem((1,)), sem((2, NY - 1)),
            sem((1,)), sem((1,)),
            sem((6,)), sem((3,)), sem((3,)),
            sem((1,)), sem((2,)),
            sem((1,)), sem((2,)),
            sem((7,)), sem((2,)), sem((2,)),
        ],
        compiler_params=pltpu.CompilerParams(
            collective_id=0, has_side_effects=True, vmem_limit_bytes=60 * 2**20
        ),
        name="prefix_attention_backward",
    )(queries, roll_kv, prefix_kv, grad_seed, lengths, rewards)
    return pl.pallas_call(
        emit,
        out_shape=(
            jax.ShapeDtypeStruct(queries.shape, BF16),
            jax.ShapeDtypeStruct(roll_kv.shape, BF16),
            jax.ShapeDtypeStruct(prefix_kv.shape, BF16),
        ),
        in_specs=[hbm] * 3,
        out_specs=[hbm] * 3,
        scratch_shapes=[
            vmem((2, ncol, 16, HD), BF16), vmem((2, 8, 512), F32), vmem(prefix_kv.shape, BF16),
            vmem(queries.shape, BF16),
            vmem(roll_kv.shape, BF16), sem((6,)), sem((6,)),
        ],
        compiler_params=pltpu.CompilerParams(vmem_limit_bytes=60 * 2**20),
        name="emit",
    )(*grads)


def solution(mesh):
    rows = ("group", "rollout")
    return jax.shard_map(
        local,
        mesh=mesh,
        in_specs=(
            P(rows, None), P(None, rows, None), P(rows, None, None), P(rows, None), P(rows), P(rows),
        ),
        out_specs=(P(rows, None), P(None, rows, None), P(rows, None, None)),
        check_vma=False,
    )
```

```python
import functools
import math

import jax
import jax.numpy as jnp
from jax import lax
from jax.experimental import pallas as pl
from jax.experimental.pallas import tpu as pltpu
from jax.sharding import PartitionSpec as P

HD = 128
GROUP = 4
NY = 4
NZ = 8
ROWS = 128
SCALE = 1.0 / math.sqrt(HD)
LOG2E = 1.4426950408889634
UNROLL = 4
MESH = pl.DeviceIdType.MESH
F32 = jnp.float32
BF16 = jnp.bfloat16
NT = (((1,), (1,)), ((), ()))
TN = (((0,), (0,)), ((), ()))


def dot(a, b, dims=(((1,), (0,)), ((), ()))):
    return lax.dot_general(a, b, dims, preferred_element_type=F32)


def kernel(
    q_hbm, rkv_hbm, pkv_hbm, do_hbm, len_hbm, rew_hbm,
    gq_ref, grkv_ref, zback,
    pkv_in, len_in, rew_in, kvblk, zrecv, kv_all, stat_own, statz, staty_own, staty,
    q_in, do_in, rkv_in, qcat, docat, e_sc, dp_sc, top_sc, sum_sc, dot_sc, p_sc, ds_sc, weights,
    ysend, yrecv, yown, zsend, gq_st, grkv_st, gq_back, grkv_back,
    zs_sem, zr_sem, ss_sem, sr_sem, ys_sem, yr_sem, sys_sem, syr_sem,
    in_sem, xs_sem, xr_sem, rys_sem, ryr_sem, rzs_sem, rzr_sem, out_sem, os_sem, or_sem,
):
    group = lax.axis_index("group")
    index = lax.axis_index("rollout")
    y = index // (2 * NZ)
    z = (index // 2) % NZ
    core = index % 2
    other = 1 - core
    prefix = NY * NZ * 16

    def device(yy, zz, cc):
        return (group, (yy * NZ + zz) * 2 + cc)

    def remote(src, dst, ssem, rsem, where):
        return pltpu.make_async_remote_copy(
            src_ref=src, dst_ref=dst, send_sem=ssem, recv_sem=rsem,
            device_id=where, device_id_type=MESH,
        )

    column = [(d, e) for d in reversed(range(NZ)) for e in range(2) if d or e]
    half = NZ // 2
    close = [(d, e) for d, e in column if d <= half]

    def peer(d, e):
        return device(y, z ^ d, core ^ e)

    barrier = pltpu.get_barrier_semaphore()
    for d, e in close:
        pl.semaphore_signal(barrier, inc=1, device_id=peer(d, e), device_id_type=MESH)
    for d in range(1, NY):
        pl.semaphore_signal(
            barrier, inc=1, device_id=device((y + d) % NY, z, core), device_id_type=MESH
        )

    my_q = pl.multiple_of(core * 1024, 1024)
    other_q = pl.multiple_of(other * 1024, 1024)
    my_kv = pl.multiple_of(core * 256, 256)
    other_kv = pl.multiple_of(other * 256, 256)
    loads = [
        pltpu.make_async_copy(q_hbm.at[:, pl.ds(my_q, 1024)], q_in.at[core], in_sem.at[0]),
        pltpu.make_async_copy(do_hbm.at[:, pl.ds(my_q, 1024)], do_in.at[core], in_sem.at[1]),
        pltpu.make_async_copy(rkv_hbm.at[:, :, pl.ds(my_kv, 256)], rkv_in.at[core], in_sem.at[2]),
    ]
    small = [
        pltpu.make_async_copy(pkv_hbm, pkv_in, in_sem.at[3]),
        pltpu.make_async_copy(len_hbm, len_in, in_sem.at[4]),
        pltpu.make_async_copy(rew_hbm, rew_in, in_sem.at[5]),
    ]
    for load in small + loads:
        load.start()
    for load in small:
        load.wait()

    pair = pkv_in[...].astype(F32)
    own_k = pair[:, 0, :]
    own_v = pair[:, 1, :]
    for hd in range(2):
        for cc in range(2):
            cols = slice(cc * 256 + hd * HD, cc * 256 + hd * HD + HD)
            kvblk[hd, cc] = jnp.concatenate([own_k[:, cols], own_v[:, cols]], axis=0).astype(BF16)
        zrecv[hd, z * 2 + core] = kvblk[hd, core]

    lane = lax.broadcasted_iota(jnp.int32, (1, 128), 1)
    reward = rew_in[0].astype(F32)
    length = len_in[0].astype(F32)
    stat = jnp.where(
        lane == 0, reward, jnp.where(lane == 1, reward * reward, jnp.where(lane == 2, length, 0.0))
    )
    stat_own[0] = stat
    statz[z * 2 + core] = stat

    pl.semaphore_wait(barrier, len(close) + NY - 1)

    def column_send(hd):
        for d, e in close:
            remote(
                kvblk.at[hd, core ^ e], zrecv.at[hd, z * 2 + core], zs_sem.at[0], zr_sem.at[hd, d],
                peer(d, e),
            ).start()

    column_send(0)
    for d, e in close:
        remote(
            stat_own.at[0], statz.at[z * 2 + core], ss_sem.at[0], sr_sem.at[d // half], peer(d, e)
        ).start()
    column_send(1)
    partner = device(y, z, other)
    xcopies = [
        remote(q_hbm.at[:, pl.ds(other_q, 1024)], q_in.at[core], xs_sem.at[0], xr_sem.at[0], partner),
        remote(
            rkv_hbm.at[:, :, pl.ds(other_kv, 256)], rkv_in.at[core], xs_sem.at[1], xr_sem.at[1], partner
        ),
        remote(do_hbm.at[:, pl.ds(other_q, 1024)], do_in.at[core], xs_sem.at[2], xr_sem.at[2], partner),
    ]
    for copy in xcopies:
        copy.start()

    def row_send(hd, chips):
        for d in chips:
            zz = z ^ d
            landed = zrecv.at[hd, pl.ds(zz * 2, 2)] if d else zrecv.at[hd, pl.ds(z * 2 + other, 1)]
            if d != half:
                remote(landed, landed, zs_sem.at[0], zr_sem.at[hd, d], peer(d or 1, 0)).wait_recv()
            first = zrecv[hd, zz * 2].astype(F32)
            second = zrecv[hd, zz * 2 + 1].astype(F32)
            at = pl.ds(pl.multiple_of(zz * 16, 16), 16)
            kv_all[hd, 0, 0, at, :] = jnp.concatenate([first[:8], second[:8]], axis=0).astype(BF16)
            kv_all[hd, 1, 0, at, :] = jnp.concatenate([first[8:], second[8:]], axis=0).astype(BF16)
            for k in (2, 1, 3):
                remote(
                    kv_all.at[hd, :, 0, at, :], kv_all.at[hd, :, k, at, :], ys_sem.at[0],
                    yr_sem.at[hd, k - 1], device((y + k) % NY, z, core),
                ).start()

    def block(hd, slot):
        cols = slice(hd * HD, (hd + 1) * HD)

        def strip(s, carry):
            if slot == NY:
                k_rows = rkv_in[s // 2, 0, :, cols]
                v_rows = rkv_in[s // 2, 1, :, cols]
            else:
                k_rows = kv_all[hd, 0, slot]
                v_rows = kv_all[hd, 1, slot]
            scores = dot(k_rows, qcat[hd, s], NT)
            if slot == NY:
                key = lax.broadcasted_iota(jnp.int32, (ROWS, 256), 0)
                query = lax.broadcasted_iota(jnp.int32, (ROWS, 256), 1) % ROWS
                scores = jnp.where(key <= query, scores, -1e30)
            grad_soft = dot(v_rows, docat[hd, s], NT)
            top = jnp.max(scores, axis=0, keepdims=True)
            powers = jnp.exp2((scores - top) * (SCALE * LOG2E))
            e_sc[hd, s, slot] = powers
            dp_sc[hd, s, slot] = grad_soft
            top_sc[hd, s, slot] = top
            sum_sc[hd, s, slot] = jnp.sum(powers, axis=0, keepdims=True)
            dot_sc[hd, s, slot] = jnp.sum(powers * grad_soft, axis=0, keepdims=True)
            return carry

        lax.fori_loop(0, 4, strip, 0, unroll=UNROLL)

    for load in loads:
        load.wait()
    for copy in xcopies:
        copy.wait_recv()
    for hd in range(2):
        for j in range(2):
            for g in range(GROUP):
                col = hd * 512 + g * HD
                at = slice((g % 2) * ROWS, (g % 2 + 1) * ROWS)
                qcat[hd, 2 * j + g // 2, at, :] = q_in[j, :, col : col + HD]
                docat[hd, 2 * j + g // 2, at, :] = do_in[j, :, col : col + HD]
    block(0, NY)
    block(1, NY)
    mirror = pl.ds((z ^ half) * 2, 2)

    def pass_on(hd):
        block_pair = zrecv.at[hd, mirror]
        remote(block_pair, block_pair, zs_sem.at[0], zr_sem.at[hd, half], peer(half, 0)).wait_recv()
        for d in reversed(range(1, half)):
            remote(block_pair, block_pair, zs_sem.at[0], zr_sem.at[hd, half + d], peer(d, 0)).start()

    pass_on(0)
    stat_pair = statz.at[mirror]
    remote(stat_pair, stat_pair, ss_sem.at[0], sr_sem.at[1], peer(half, 0)).wait_recv()
    for d in reversed(range(1, half)):
        remote(stat_pair, stat_pair, ss_sem.at[0], sr_sem.at[0], peer(d, 0)).start()
    pass_on(1)
    row_send(0, range(half))
    row_send(1, range(half))
    row_send(0, range(half, NZ))
    all_but_one = statz.at[pl.ds(0, len(column))]
    stats = remote(all_but_one, all_but_one, ss_sem.at[0], sr_sem.at[0], peer(1, 0))
    unmirrored = statz.at[pl.ds(0, len(column) - 2)]
    remote(unmirrored, unmirrored, ss_sem.at[0], sr_sem.at[0], peer(1, 0)).wait_recv()
    column_sum = jnp.sum(statz[...], axis=0)
    staty_own[0] = column_sum
    staty[y] = column_sum
    for k in range(1, NY):
        remote(
            staty_own.at[0], staty.at[y], sys_sem.at[0], syr_sem.at[0], device((y + k) % NY, z, core)
        ).start()

    row_send(1, range(half, NZ))
    block(0, 0)
    block(1, 0)

    def row_wait(hd, k):
        remote(
            kv_all.at[hd, :, 0], kv_all.at[hd, :, k], ys_sem.at[0], yr_sem.at[hd, k - 1],
            device((y + NY - k) % NY, z, core),
        ).wait_recv()

    for k in (1, 3, 2):
        row_wait(0, k)
        block(0, k)

    next_row = device((y + 1) % NY, z, core)
    other_rows = staty.at[pl.ds(0, NY - 1)]
    row_stats = remote(other_rows, other_rows, sys_sem.at[0], syr_sem.at[0], next_row)
    row_stats.wait_recv()
    totals = jnp.sum(staty[...], axis=0)
    rollouts = float(2 * NY * NZ)
    mean = totals[:, 0:1] / rollouts
    var = totals[:, 1:2] / rollouts - mean * mean
    divisor = jnp.sqrt(var) + 1.0
    norm = float(2 * NY * NZ * ROWS) / totals[:, 2:3]
    step = (lax.broadcasted_iota(jnp.int32, (1, 256), 1) % ROWS).astype(F32)
    for j in range(2):
        own = statz[z * 2 + j]
        weight = (own[:, 0:1] - mean) / divisor * norm
        weights[j] = jnp.where(step < own[:, 2:3], weight, 0.0)

    def finish(hd):
        def strip(s, carry):
            tops = [top_sc[hd, s, b] for b in range(NY + 1)]
            top = functools.reduce(jnp.maximum, tops)
            factors = [jnp.exp2((t - top) * (SCALE * LOG2E)) for t in tops]
            total = sum(sum_sc[hd, s, b] * factors[b] for b in range(NY + 1))
            inverse = 1.0 / total
            row_dot = sum(dot_sc[hd, s, b] * factors[b] for b in range(NY + 1)) * inverse
            scaled = weights[s // 2] * inverse
            at = pl.ds(pl.multiple_of(s * 256, 256), 256)
            for b in range(NY + 1):
                soft = e_sc[hd, s, b] * (factors[b] * scaled)
                rows = slice(b * ROWS, (b + 1) * ROWS)
                p_sc[hd, rows, at] = soft.astype(BF16)
                ds_sc[hd, rows, at] = (soft * (dp_sc[hd, s, b] - row_dot)).astype(BF16)
            return carry

        lax.fori_loop(0, 4, strip, 0, unroll=4)

    def prefix_grads(hd, kind):
        held, rows = (ds_sc, qcat) if kind == 0 else (p_sc, docat)
        grad = dot(held[hd, :prefix, :], rows[hd].reshape(1024, HD))
        if kind == 0:
            grad = grad * SCALE
        yown[hd, kind] = grad[:ROWS]
        for k in (2, 1, 3):
            ysend[hd, kind, k - 1] = grad[k * ROWS : (k + 1) * ROWS].astype(BF16)
            remote(
                ysend.at[hd, kind, k - 1], yrecv.at[hd, kind, k - 1], rys_sem.at[0], ryr_sem.at[hd],
                device((y + NY - k) % NY, z, core),
            ).start()

    def local_grads(hd):
        cols = slice(hd * HD, (hd + 1) * HD)
        for j in range(2):
            qs = qcat[hd, 2 * j : 2 * j + 2].reshape(512, HD)
            dos = docat[hd, 2 * j : 2 * j + 2].reshape(512, HD)
            at = slice(j * 512, j * 512 + 512)
            grkv_st[j, 0, :, cols] = (dot(ds_sc[hd, prefix:, at], qs) * SCALE).astype(BF16)
            grkv_st[j, 1, :, cols] = dot(p_sc[hd, prefix:, at], dos).astype(BF16)

        def query_strip(s, carry):
            j = s // 2
            at = pl.ds(pl.multiple_of(s * 256, 256), 256)
            kp = kv_all[hd, 0].reshape(prefix, HD)
            ko = rkv_in[j, 0, :, cols]
            grad = dot(kp, ds_sc[hd, :prefix, at], TN) + dot(ko, ds_sc[hd, prefix:, at], TN)
            grad = (grad * SCALE).T.astype(BF16)
            for g in range(2):
                col = pl.multiple_of(hd * 512 + (s % 2) * 256 + g * HD, HD)
                gq_st[j, :, pl.ds(col, HD)] = grad[g * ROWS : (g + 1) * ROWS]
            return carry

        lax.fori_loop(0, 4, query_strip, 0, unroll=UNROLL)

    def row_sums(hd):
        remote(ysend.at[hd], yrecv.at[hd], rys_sem.at[0], ryr_sem.at[hd], next_row).wait_recv()
        sums = [
            yown[hd, i]
            + (yrecv[hd, i, 0].astype(F32) + yrecv[hd, i, 1].astype(F32) + yrecv[hd, i, 2].astype(F32))
            for i in range(2)
        ]
        for zz in range(NZ):
            for cc in range(2):
                at = slice(zz * 16 + cc * 8, zz * 16 + cc * 8 + 8)
                zsend[hd, zz * 2 + cc] = jnp.concatenate([sums[0][at], sums[1][at]], axis=0).astype(BF16)
        own_share = pltpu.make_async_copy(
            zsend.at[hd, z * 2 + core], zback.at[hd, z * 2 + core], out_sem.at[5 + hd]
        )
        own_share.start()
        outs.append(own_share)
        for d, e in column:
            remote(
                zsend.at[hd, (z ^ d) * 2 + (core ^ e)], zback.at[hd, z * 2 + core], rzs_sem.at[0],
                rzr_sem.at[hd], peer(d, e),
            ).start()

    for hd in range(2):
        if hd == 1:
            for k in (1, 3, 2):
                row_wait(1, k)
                block(1, k)
        finish(hd)
        prefix_grads(hd, 1)
        prefix_grads(hd, 0)
    local_grads(0)
    local_grads(1)
    outs = [
        pltpu.make_async_copy(gq_st.at[core], gq_ref.at[:, pl.ds(my_q, 1024)], out_sem.at[0]),
        pltpu.make_async_copy(grkv_st.at[core], grkv_ref.at[:, :, pl.ds(my_kv, 256)], out_sem.at[1]),
    ]
    ocopies = [
        remote(gq_st.at[other], gq_back, os_sem.at[0], or_sem.at[0], partner),
        remote(grkv_st.at[other], grkv_back, os_sem.at[1], or_sem.at[1], partner),
    ]
    for copy in ocopies + outs:
        copy.start()
    row_sums(0)
    row_sums(1)
    backs = [
        pltpu.make_async_copy(gq_back, gq_ref.at[:, pl.ds(other_q, 1024)], out_sem.at[3]),
        pltpu.make_async_copy(grkv_back, grkv_ref.at[:, :, pl.ds(other_kv, 256)], out_sem.at[4]),
    ]
    for copy, back in zip(ocopies, backs):
        copy.wait_recv()
        back.start()
    outs = outs + backs

    for copy in outs:
        copy.wait()
    for copy in ocopies + xcopies:
        copy.wait_send()
    stats.wait_send()
    row_stats.wait_send()
    for held, sem in (
        (zrecv.at[:, pl.ds(0, len(column))], zs_sem.at[0]),
        (kv_all.at[:, :, pl.ds(1, NY - 1)], ys_sem.at[0]),
        (ysend, rys_sem.at[0]),
        (zsend.at[:, pl.ds(0, len(column))], rzs_sem.at[0]),
    ):
        remote(held, held, sem, sem, next_row).wait_send()
    for hd in range(2):
        landed = zback.at[hd, pl.ds(0, len(column))]
        remote(landed, landed, rzs_sem.at[0], rzr_sem.at[hd], peer(1, 0)).wait_recv()


def emit(gq_from, grkv_from, shares_from, gq_to, grkv_to, gp_to, shares, sums, pairs, gq, grkv, fetch_sem, put_sem):
    ways = [(shares_from, shares, None), (grkv_from, grkv, grkv_to)]
    for i in range(4):
        at = pl.ds(i * 32, 32)
        ways.append((gq_from.at[at], gq.at[at], gq_to.at[at]))
    fetches = [pltpu.make_async_copy(way[0], way[1], fetch_sem.at[i]) for i, way in enumerate(ways)]
    for fetch in fetches:
        fetch.start()
    puts = []
    for i in range(1, len(ways)):
        fetches[i].wait()
        puts.append(pltpu.make_async_copy(ways[i][1], ways[i][2], put_sem.at[i]))
        puts[-1].start()
    fetches[0].wait()
    for cc in range(2):
        for hd in range(2):
            total = shares[hd, cc].astype(F32)
            for zz in range(1, NZ):
                total = total + shares[hd, zz * 2 + cc].astype(F32)
            cols = slice(cc * 256 + hd * HD, cc * 256 + (hd + 1) * HD)
            sums[0, :, cols] = total[:8]
            sums[1, :, cols] = total[8:]
    pairs[...] = jnp.stack([sums[0], sums[1]], axis=1).astype(BF16)
    puts.append(pltpu.make_async_copy(pairs, gp_to, put_sem.at[0]))
    puts[-1].start()
    for put in puts:
        put.wait()


def local(queries, roll_kv, prefix_kv, grad_seed, lengths, rewards):
    prefix = NY * NZ * 16
    keys = prefix + ROWS
    near = NZ * 16
    vmem = pltpu.VMEM
    sem = pltpu.SemaphoreType.DMA
    hbm = pl.BlockSpec(memory_space=pltpu.HBM)
    ncol = 2 * NZ
    grads = pl.pallas_call(
        kernel,
        out_shape=(
            jax.ShapeDtypeStruct(queries.shape, BF16),
            jax.ShapeDtypeStruct(roll_kv.shape, BF16),
            jax.ShapeDtypeStruct((2, ncol, 16, HD), BF16),
        ),
        in_specs=[hbm] * 6,
        out_specs=(hbm, hbm, hbm),
        scratch_shapes=[
            vmem(prefix_kv.shape, BF16),
            pltpu.SMEM((1,), jnp.int32),
            pltpu.SMEM((1,), jnp.int32),
            vmem((2, 2, 16, HD), BF16),
            vmem((2, ncol, 16, HD), BF16),
            vmem((2, 2, NY, near, HD), BF16),
            vmem((1, 1, 128), F32),
            vmem((ncol, 1, 128), F32),
            vmem((1, 1, 128), F32),
            vmem((NY, 1, 128), F32),
            vmem((2, ROWS, 1024), BF16),
            vmem((2, ROWS, 1024), BF16),
            vmem((2, 2, ROWS, 256), BF16),
            vmem((2, 4, 256, HD), BF16),
            vmem((2, 4, 256, HD), BF16),
            vmem((2, 4, NY + 1, ROWS, 256), F32),
            vmem((2, 4, NY + 1, ROWS, 256), F32),
            vmem((2, 4, NY + 1, 1, 256), F32),
            vmem((2, 4, NY + 1, 1, 256), F32),
            vmem((2, 4, NY + 1, 1, 256), F32),
            vmem((2, keys, 1024), BF16),
            vmem((2, keys, 1024), BF16),
            vmem((2, 1, 256), F32),
            vmem((2, 2, NY - 1, near, HD), BF16),
            vmem((2, 2, NY - 1, near, HD), BF16),
            vmem((2, 2, near, HD), F32),
            vmem((2, ncol, 16, HD), BF16),
            vmem((2, ROWS, 1024), BF16),
            vmem((2, 2, ROWS, 256), BF16),
            vmem((ROWS, 1024), BF16),
            vmem((2, ROWS, 256), BF16),
            sem((1,)), sem((2, NZ)),
            sem((1,)), sem((2,)),
            sem((1,)), sem((2, NY - 1)),
            sem((1,)), sem((1,)),
            sem((6,)), sem((3,)), sem((3,)),
            sem((1,)), sem((2,)),
            sem((1,)), sem((2,)),
            sem((7,)), sem((2,)), sem((2,)),
        ],
        compiler_params=pltpu.CompilerParams(
            collective_id=0, has_side_effects=True, vmem_limit_bytes=60 * 2**20
        ),
        name="prefix_attention_backward",
    )(queries, roll_kv, prefix_kv, grad_seed, lengths, rewards)
    return pl.pallas_call(
        emit,
        out_shape=(
            jax.ShapeDtypeStruct(queries.shape, BF16),
            jax.ShapeDtypeStruct(roll_kv.shape, BF16),
            jax.ShapeDtypeStruct(prefix_kv.shape, BF16),
        ),
        in_specs=[hbm] * 3,
        out_specs=[hbm] * 3,
        scratch_shapes=[
            vmem((2, ncol, 16, HD), BF16), vmem((2, 8, 512), F32), vmem(prefix_kv.shape, BF16),
            vmem(queries.shape, BF16),
            vmem(roll_kv.shape, BF16), sem((6,)), sem((6,)),
        ],
        compiler_params=pltpu.CompilerParams(vmem_limit_bytes=60 * 2**20),
        name="emit",
    )(*grads)


def solution(mesh):
    rows = ("group", "rollout")
    return jax.shard_map(
        local,
        mesh=mesh,
        in_specs=(
            P(rows, None), P(None, rows, None), P(rows, None, None), P(rows, None), P(rows), P(rows),
        ),
        out_specs=(P(rows, None), P(None, rows, None), P(rows, None, None)),
        check_vma=False,
    )
```
